32 devices in a mesh: batch: 4 (over x, core), mem: 8 (over z, y).
Axes of the slice: x: 2, y: 2, z: 4, core: 2. Of those that a mesh axis runs over, the one named last changes fastest.
Arguments:
- inputs: bfloat16 [4, 8192, 512], P('batch', 'mem'), may hold values from -6 to 6
- cotangent: bfloat16 [4, 8192, 512], P('batch', 'mem'), may hold values from -6 to 6
- memory: bfloat16 [4, 1024, 512], P('batch', 'mem'), may hold values from -6 to 6
- passage_ids: int32 [4, 1024], P('batch', 'mem'), may hold values from 0 to 7, never falling along the last dimension, each value on 1 to 256 neighbouring positions
- retrieved: int32 [4, 64, 4], P('batch', 'mem'), may hold values from 0 to 7, as said below
- task_ids: int32 [4, 64], P('batch', 'mem'), may hold values from 0 to 2
- target_lens: int32 [4, 64], P('batch', 'mem'), may hold values from 1 to 128
- encoder_gain: float32 [512], replicated, may hold values from 0.5 to 1.5
- self_gain: float32 [512], replicated, may hold values from 0.5 to 1.5
- cross_gain: float32 [512], replicated, may hold values from 0.5 to 1.5
- feed_gain: float32 [512], replicated, may hold values from 0.5 to 1.5
- self_query: bfloat16 [512, 512], replicated, may hold values from -0.0625 to 0.0625
- self_key: bfloat16 [512, 512], replicated, may hold values from -0.25 to 0.25
- self_value: bfloat16 [512, 512], replicated, may hold values from -0.25 to 0.25
- self_output: bfloat16 [512, 512], replicated, may hold values from -0.375 to 0.375
- cross_query: bfloat16 [512, 512], replicated, may hold values from -0.0625 to 0.0625
- cross_key: bfloat16 [512, 512], replicated, may hold values from -0.25 to 0.25
- cross_value: bfloat16 [512, 512], replicated, may hold values from -0.25 to 0.25
- cross_output: bfloat16 [512, 512], replicated, may hold values from -0.75 to 0.75
- inner_weight: bfloat16 [512, 2048], replicated, may hold values from -0.25 to 0.25
- outer_weight: bfloat16 [2048, 512], replicated, may hold values from -0.1875 to 0.1875
Outputs:
- layer_out: bfloat16 [4, 8192, 512], P('batch', 'mem')
- grad_inputs: float32 [4, 8192, 512], P('batch', 'mem')
- grad_memory: float32 [4, 1024, 512], P('batch', 'mem')
- grad_encoder_gain: float32 [512], replicated
- grad_self_gain: float32 [512], replicated
- grad_cross_gain: float32 [512], replicated
- grad_feed_gain: float32 [512], replicated
- grad_self_query: float32 [512, 512], replicated
- grad_self_key: float32 [512, 512], replicated
- grad_self_value: float32 [512, 512], replicated
- grad_self_output: float32 [512, 512], replicated
- grad_cross_query: float32 [512, 512], replicated
- grad_cross_key: float32 [512, 512], replicated
- grad_cross_value: float32 [512, 512], replicated
- grad_cross_output: float32 [512, 512], replicated
- grad_inner_weight: float32 [512, 2048], replicated
- grad_outer_weight: float32 [2048, 512], replicated
The draws below stay inside these ranges and needn't reach their ends.
Inputs may be any that keep to these rules, and one draw needn't show every extreme that they name: `passage_ids`: along the 1024 rows of a group the passage id never falls; each of the 8 passages holds 1 to 256 consecutive rows, and some passage exactly 256. `retrieved`: the 4 passages that one query reads are distinct passages of its own group.
All inputs are finite; a program needn't handle non-finite values.
Results may differ from the reference program's by a relative error of at most 0.02.
Values may be sent and summed in bfloat16 or wider, within the bound.
No kernel may reach another device: no remote copies, remote signals or barrier semaphores. Data moves between devices by JAX's collectives and lax.ppermute only.
A program may use at most 320 MiB of HBM per device.

```python
import math
import jax
import jax.numpy as jnp
import numpy as np
from jax import lax

D = 512
HEADS = 8
HDIM = 64
FF = 2048
SEQ = 128
PLEN = 256
PASS = 4
GROUPS = 4
QUERIES = 64
TOKENS = 8192
NMEM = 1024
PASSAGES = 8
SLOTS = 1024


def draw_retrieved(key, part):
    query_keys = jax.random.split(key, GROUPS * QUERIES)

    def pick_passages(single_key):
        return jax.random.permutation(single_key, PASSAGES)[:PASS]
    picks = jax.vmap(pick_passages)(query_keys)
    return picks.reshape(GROUPS, QUERIES, PASS).astype(jnp.int32)


def set_ends(drawn, own_key, low, high):
    place = [jax.random.randint(jax.random.fold_in(own_key, axis), (), 0, length) for axis, length in enumerate(drawn.shape)]
    widest = drawn.shape.index(max(drawn.shape))
    neighbour = place[:widest] + [(place[widest] + 1) % drawn.shape[widest]] + place[widest + 1:]
    return drawn.at[tuple(place)].set(low).at[tuple(neighbour)].set(high)


def level_of(key, shape, pieces, least, top_value):
    loudness = 1.0
    for axis_at, parts in pieces:
        draws = jax.random.uniform(jax.random.fold_in(jax.random.fold_in(key, 6), axis_at), (parts,), jnp.float32, least / len(pieces), top_value / len(pieces))
        loudness = loudness * jnp.repeat(jnp.exp(draws), shape[axis_at] // parts).reshape((-1,) + (1,) * (len(shape) - 1 - axis_at))
    return loudness


def length_profile(number_of, total, reach, slope):
    portions = [(1 << 20) // math.isqrt(grade ** slope) + 1 for grade in range(2, number_of + 1)]
    spare, given = total - reach - (number_of - 1), [1] * (number_of - 1)
    while spare > 0:
        candidates = [i for i in range(number_of - 1) if given[i] < reach]
        pool, remaining = sum([portions[i] for i in candidates]), spare
        for i in candidates:
            more = min(reach - given[i], max(1, remaining * portions[i] // pool), spare)
            given[i] = given[i] + more
            spare = spare - more
    return np.array([reach] + given)


def ragged(own_key, number_of, total, limit, slope):
    if number_of == 2:
        one = jax.random.randint(own_key, (), max(1, total - limit), min(limit, total - 1) + 1)
        return jnp.stack([one, total - one])
    sizes = jnp.asarray(length_profile(number_of, total, limit, slope), jnp.int32)
    twos = (number_of - 1) // 2
    donor, sink = sizes[1:1 + 2 * twos:2], sizes[2:2 + 2 * twos:2]
    room = jnp.minimum(donor - 1, limit - sink)
    shifted = jax.random.randint(jax.random.fold_in(own_key, 1), (twos,), 0, 1 << 20) % (room + 1)
    sizes = sizes.at[1:1 + 2 * twos:2].set(donor - shifted).at[2:2 + 2 * twos:2].set(sink + shifted)
    return sizes[jax.random.permutation(jax.random.fold_in(own_key, 2), number_of)]


def normal_values(rng, shape, scale, most, cuts=(), held_as=jnp.bfloat16):
    drawn = scale * jax.random.normal(rng, shape, jnp.float32)
    if cuts:
        drawn = drawn * level_of(rng, shape, cuts, -0.22, 0.18)
    return jnp.clip(drawn, -most, most).astype(held_as)


def setup_inputs(seed: int = 0) -> dict:
    arg_keys = jax.random.split(jax.random.key(seed), 22)
    inputs = normal_values(arg_keys[0], (GROUPS, TOKENS, D), 1.0, 6.0, ((0, 4), (1, 8)))
    cotangent = normal_values(arg_keys[1], (GROUPS, TOKENS, D), 1.0, 6.0, ((0, 4), (1, 8)))
    memory = normal_values(arg_keys[2], (GROUPS, NMEM, D), 1.0, 6.0, ((0, 4), (1, 8)))
    passage_ids = jax.vmap(lambda own: jnp.searchsorted(jnp.cumsum(ragged(own, PASSAGES, NMEM, PLEN, 1)), jnp.arange(NMEM), side="right"))(jax.random.split(arg_keys[3], GROUPS)).reshape((GROUPS, NMEM)).astype(jnp.int32)
    retrieved = draw_retrieved(jax.random.fold_in(arg_keys[21], 71), 0)
    task_ids = set_ends(jax.random.randint(arg_keys[5], (GROUPS, QUERIES), 0, 3), jax.random.fold_in(arg_keys[5], 1), 0, 2).astype(jnp.int32)
    target_lens = set_ends(jax.random.randint(arg_keys[6], (GROUPS, QUERIES), 1, SEQ + 1), jax.random.fold_in(arg_keys[6], 1), 1, SEQ).astype(jnp.int32)
    encoder_gain = jnp.clip(1.0 + 0.1 * jax.random.normal(arg_keys[7], (D,), jnp.float32), 0.5, 1.5)
    self_gain = jnp.clip(1.0 + 0.1 * jax.random.normal(arg_keys[8], (D,), jnp.float32), 0.5, 1.5)
    cross_gain = jnp.clip(1.0 + 0.1 * jax.random.normal(arg_keys[9], (D,), jnp.float32), 0.5, 1.5)
    feed_gain = jnp.clip(1.0 + 0.1 * jax.random.normal(arg_keys[10], (D,), jnp.float32), 0.5, 1.5)
    self_query = normal_values(arg_keys[11], (D, D), (D * 16) ** -0.5, 0.0625)
    self_key = normal_values(arg_keys[12], (D, D), D ** -0.5, 0.25)
    self_value = normal_values(arg_keys[13], (D, D), D ** -0.5, 0.25)
    self_output = normal_values(arg_keys[14], (D, D), (D // 2) ** -0.5, 0.375)
    cross_query = normal_values(arg_keys[15], (D, D), (D * 16) ** -0.5, 0.0625)
    cross_key = normal_values(arg_keys[16], (D, D), D ** -0.5, 0.25)
    cross_value = normal_values(arg_keys[17], (D, D), D ** -0.5, 0.25)
    cross_output = normal_values(arg_keys[18], (D, D), (D // 8) ** -0.5, 0.75)
    inner_weight = normal_values(arg_keys[19], (D, FF), D ** -0.5, 0.25)
    outer_weight = normal_values(arg_keys[20], (FF, D), (FF // 2) ** -0.5, 0.1875)
    return dict(inputs=inputs, cotangent=cotangent, memory=memory, passage_ids=passage_ids, retrieved=retrieved, task_ids=task_ids, target_lens=target_lens, encoder_gain=encoder_gain, self_gain=self_gain, cross_gain=cross_gain, feed_gain=feed_gain, self_query=self_query, self_key=self_key, self_value=self_value, self_output=self_output, cross_query=cross_query, cross_key=cross_key, cross_value=cross_value, cross_output=cross_output, inner_weight=inner_weight, outer_weight=outer_weight)


EPSILON = 1e-06
HIGHEST = lax.Precision.HIGHEST

@jax.custom_vjp
def low(v):
    return lax.optimization_barrier(v.astype(jnp.bfloat16)).astype(jnp.float32)

@jax.custom_vjp
def low_back(v):
    return v

def low_keep(v):
    return (low(v), None)

def low_pass(kept, grad):
    return (grad,)

def back_keep(v):
    return (v, None)

def back_low(kept, grad):
    return (low(grad),)
low.defvjp(low_keep, low_pass)
low_back.defvjp(back_keep, back_low)

def matmul(former, latter):
    return jnp.dot(former, latter, precision=HIGHEST)

def rms_norm(values, norm_gain):
    return values * lax.rsqrt(lax.optimization_barrier(jnp.mean(values * values, axis=-1, keepdims=True)) + EPSILON) * norm_gain

def attention(queries, key_rows, value_rows, visible):
    row_count = queries.shape[0]
    query_heads = queries.reshape(row_count, HEADS, HDIM)
    key_heads = key_rows.reshape(key_rows.shape[0], HEADS, HDIM)
    value_heads = value_rows.reshape(value_rows.shape[0], HEADS, HDIM)
    raw_scores = jnp.einsum('she,lhe->hsl', query_heads, key_heads, precision=HIGHEST)
    seen = jnp.broadcast_to(visible[None], raw_scores.shape)
    scores = low_back(jnp.where(seen, raw_scores, 0.0))
    largest = lax.optimization_barrier(jnp.max(jnp.where(seen, scores, lax.optimization_barrier(jnp.min(scores, axis=-1, keepdims=True))), axis=-1, keepdims=True))
    powered = jnp.where(seen, jnp.exp(scores - largest), 0.0)
    chances = low(powered / lax.optimization_barrier(jnp.sum(powered, axis=-1, keepdims=True)))
    blended = jnp.einsum('hsl,lhe->she', chances, value_heads, precision=HIGHEST)
    return low_back(low(blended.reshape(row_count, HEADS * HDIM)))

def passage_slots(group_ids, chosen):
    passage_marks = jnp.arange(PASSAGES, dtype=jnp.int32)
    starts = lax.optimization_barrier(jnp.sum((group_ids[None, :] < passage_marks[:, None]).astype(jnp.int32), axis=1, dtype=jnp.int32))
    counts = lax.optimization_barrier(jnp.sum((group_ids[None, :] == passage_marks[:, None]).astype(jnp.int32), axis=1, dtype=jnp.int32))
    offsets = jnp.arange(PLEN, dtype=jnp.int32)
    first_row = jnp.take(starts, chosen.astype(jnp.int32), axis=0).astype(jnp.int32)
    extent = jnp.take(counts, chosen.astype(jnp.int32), axis=0).astype(jnp.int32)
    slot_rows = jnp.minimum(first_row[..., None] + offsets, NMEM - 1).astype(jnp.int32)
    slot_visible = offsets < extent[..., None]
    return (slot_rows.reshape(QUERIES, SLOTS), slot_visible.reshape(QUERIES, SLOTS))

def token_mask(group_tasks, group_lens):
    limits = jnp.minimum(group_lens, SEQ - group_tasks * (SEQ // 4)).astype(jnp.int32)
    return jnp.arange(SEQ, dtype=jnp.int32)[None, :] < limits[:, None]

def group_forward(params, token_rows, memory_rows, slot_rows, slot_visible):
    encoder_gain, self_gain, cross_gain, feed_gain, self_query, self_key, self_value, self_output, cross_query, cross_key, cross_value, cross_output, inner_weight, outer_weight = params
    memory_normed = low(rms_norm(memory_rows, encoder_gain))
    memory_keys = low(matmul(memory_normed, cross_key))
    memory_values = low(matmul(memory_normed, cross_value))
    causal = jnp.tril(jnp.ones((SEQ, SEQ), dtype=bool))

    def query_step(sequence, rows_taken, visible_slots):
        self_normed = low(rms_norm(sequence, self_gain))
        self_queries = low_back(low(matmul(self_normed, self_query)))
        self_keys = low_back(low(matmul(self_normed, self_key)))
        self_values = low_back(low(matmul(self_normed, self_value)))
        self_attended = attention(self_queries, self_keys, self_values, causal)
        after_self = sequence + low_back(matmul(self_attended, self_output))
        cross_normed = low(rms_norm(after_self, cross_gain))
        cross_queries = low_back(low(matmul(cross_normed, cross_query)))
        slot_keys = jnp.take(memory_keys, rows_taken.astype(jnp.int32), axis=0)
        slot_values = jnp.take(memory_values, rows_taken.astype(jnp.int32), axis=0)
        visible = jnp.broadcast_to(visible_slots[None, :], (SEQ, SLOTS))
        cross_attended = attention(cross_queries, slot_keys, slot_values, visible)
        after_cross = after_self + low_back(matmul(cross_attended, cross_output))
        feed_normed = low(rms_norm(after_cross, feed_gain))
        pre_hidden = low_back(matmul(feed_normed, inner_weight))
        hidden = low(jax.nn.gelu(pre_hidden, approximate=True))
        return after_cross + low_back(matmul(hidden, outer_weight))

    def block_step(block_items):
        return jax.vmap(query_step)(block_items[0], block_items[1], block_items[2])
    block_size = math.gcd(QUERIES, 32)
    block_count = QUERIES // block_size
    width = token_rows.shape[1]
    shaped = (token_rows.reshape(block_count, block_size, SEQ, width), slot_rows.reshape(block_count, block_size, SLOTS), slot_visible.reshape(block_count, block_size, SLOTS))
    outputs = lax.map(jax.checkpoint(block_step), shaped)
    return outputs.reshape(TOKENS, width)

def reference(inputs, cotangent, memory, passage_ids, retrieved, task_ids, target_lens, encoder_gain, self_gain, cross_gain, feed_gain, self_query, self_key, self_value, self_output, cross_query, cross_key, cross_value, cross_output, inner_weight, outer_weight):
    params = tuple((member.astype(jnp.float32) for member in (encoder_gain, self_gain, cross_gain, feed_gain, self_query, self_key, self_value, self_output, cross_query, cross_key, cross_value, cross_output, inner_weight, outer_weight)))
    totals = tuple((jnp.zeros(member.shape, jnp.float32) for member in params))
    layer_rows_all = []
    grad_tokens_all = []
    grad_memory_all = []
    for group_index in range(GROUPS):
        slot_rows, slot_visible = passage_slots(passage_ids[group_index], retrieved[group_index])

        def forward(weights_in, tokens_in, memory_in):
            return group_forward(weights_in, tokens_in, memory_in, slot_rows, slot_visible)
        layer_rows, pullback = jax.vjp(forward, params, inputs[group_index].astype(jnp.float32), memory[group_index].astype(jnp.float32))
        live_rows = token_mask(task_ids[group_index], target_lens[group_index]).reshape(TOKENS, 1).astype(jnp.float32)
        grad_params, grad_tokens, grad_memory_rows = pullback(cotangent[group_index].astype(jnp.float32) * live_rows)
        totals = tuple((former + latter for former, latter in zip(totals, grad_params)))
        layer_rows_all.append(layer_rows)
        grad_tokens_all.append(grad_tokens)
        grad_memory_all.append(grad_memory_rows)
    return (jnp.stack(layer_rows_all).astype(jnp.bfloat16), jnp.stack(grad_tokens_all), jnp.stack(grad_memory_all), totals[0], totals[1], totals[2], totals[3], totals[4], totals[5], totals[6], totals[7], totals[8], totals[9], totals[10], totals[11], totals[12], totals[13])
```

```python
import functools

import jax
import jax.numpy as jnp
from jax import lax
from jax.experimental import pallas as pl
from jax.experimental.pallas import tpu as pltpu
from jax.sharding import PartitionSpec as P

HEADS = 8
HDIM = 64
SEQ = 128
PLEN = 256
PASS_DEV = 1
PAIRS = HEADS // 2
PAIR = 2 * HDIM

EPSILON = 1e-06
MASKED = -1e30
F32 = jnp.float32
BF16 = jnp.bfloat16
MIB = 1024 * 1024
BLOCKS = 32


def dot_nn(former, latter):
    return lax.dot_general(
        former, latter, (((1,), (0,)), ((), ())), preferred_element_type=F32
    )


def dot_tn(former, latter):
    return lax.dot_general(
        former, latter, (((0,), (0,)), ((), ())), preferred_element_type=F32
    )


def dot_nt(former, latter):
    return lax.dot_general(
        former, latter, (((1,), (1,)), ((), ())), preferred_element_type=F32
    )


def inverse_rms(values):
    return lax.rsqrt(jnp.mean(values * values, axis=-1, keepdims=True) + EPSILON)


def norm_pull(values, row_scale, norm_gain, grad_normed):
    weighted = grad_normed * norm_gain
    cubed = row_scale * row_scale * row_scale
    grad_values = row_scale * weighted - values * (
        cubed * jnp.mean(values * weighted, axis=-1, keepdims=True)
    )
    return grad_values


def head_pair_rows(values):
    lane = lax.broadcasted_iota(jnp.int32, values.shape, 1)
    zero = jnp.zeros_like(values)
    return jnp.concatenate(
        [jnp.where(lane < HDIM, values, zero), jnp.where(lane < HDIM, zero, values)], axis=0
    )


def head_pair_diagonal(values, rows):
    return jnp.concatenate([values[:HDIM, :rows], values[HDIM:, rows:]], axis=0)


def store_turned(code, value, keep_ref, send_ref, at, staged):
    staged[...] = value.astype(BF16)
    blocks = BLOCKS
    size = value.shape[0] // blocks
    for place in range(blocks):
        source = pl.ds(pl.multiple_of((place ^ code) * size, size), size)
        half = blocks // 2
        target = keep_ref if place < half else send_ref
        start = (place % half) * size
        target[at, start : start + size, :] = staged[source, :]


def call(body, name, grid, in_specs, out_specs, out_shape, scratch=(), prefetch=0, vmem=56):
    return pl.pallas_call(
        body,
        name=name,
        grid_spec=pltpu.PrefetchScalarGridSpec(
            num_scalar_prefetch=prefetch,
            grid=grid,
            in_specs=in_specs,
            out_specs=out_specs,
            scratch_shapes=list(scratch),
        ),
        out_shape=out_shape,
        compiler_params=pltpu.CompilerParams(
            vmem_limit_bytes=vmem * MIB,
            dimension_semantics=("arbitrary",) * len(grid),
        ),
    )


def fixed(shape):
    return pl.BlockSpec(shape, lambda *_: (0,) * len(shape))


def shaped(shape, dtype):
    return jax.ShapeDtypeStruct(shape, dtype)


def memory_body(memory_ref, gain_ref, key_ref, value_ref, keys_ref, values_ref, keys_t_ref, values_t_ref):
    rows = memory_ref[...].astype(F32)
    normed = (rows * inverse_rms(rows) * gain_ref[...]).astype(BF16)
    keys_ref[...] = dot_nn(normed, key_ref[...]).astype(BF16)
    values_ref[...] = dot_nn(normed, value_ref[...]).astype(BF16)
    keys_t_ref[...] = lax.dot_general(
        key_ref[...], normed, (((0,), (1,)), ((), ())), preferred_element_type=F32
    ).astype(BF16)
    values_t_ref[...] = lax.dot_general(
        value_ref[...], normed, (((0,), (1,)), ((), ())), preferred_element_type=F32
    ).astype(BF16)


def memory_forward(memory, encoder_gain, cross_key, cross_value):
    count, width = memory.shape
    block = 512 if count % 512 == 0 else count
    row_spec = pl.BlockSpec((block, width), lambda i: (i, 0))
    column_spec = pl.BlockSpec((width, block), lambda i: (0, i))
    return call(
        memory_body,
        "memory_forward",
        (count // block,),
        [row_spec, fixed((1, width)), fixed(cross_key.shape), fixed(cross_value.shape)],
        [row_spec, row_spec, column_spec, column_spec],
        [shaped((count, width), BF16)] * 2 + [shaped((width, count), BF16)] * 2,
    )(memory, encoder_gain, cross_key, cross_value)


def memory_pull_body(
    codes_ref, memory_ref, gain_ref, key_ref, value_ref, grad_keys_ref, grad_values_ref,
    grad_normed_ref, keep_ref, send_ref, grad_key, grad_value, staged,
):
    rows = memory_ref[...].astype(F32)
    normed = (rows * inverse_rms(rows) * gain_ref[...]).astype(BF16)
    grad_keys = grad_keys_ref[...].astype(BF16)
    grad_values = grad_values_ref[...].astype(BF16)
    grad_normed = dot_nt(grad_keys, key_ref[...]) + dot_nt(grad_values, value_ref[...])
    grad_normed_ref[...] = grad_normed.astype(BF16)

    @pl.when(pl.program_id(0) == 0)
    def _():
        grad_key[...] = jnp.zeros_like(grad_key)
        grad_value[...] = jnp.zeros_like(grad_value)

    grad_key[...] += dot_tn(normed, grad_keys)
    grad_value[...] += dot_tn(normed, grad_values)

    @pl.when(pl.program_id(0) == pl.num_programs(0) - 1)
    def _():
        store_turned(codes_ref[1], grad_key[...], keep_ref, send_ref, 0, staged)
        store_turned(codes_ref[1], grad_value[...], keep_ref, send_ref, 1, staged)


def memory_backward(codes, memory, encoder_gain, cross_key, cross_value, grad_keys, grad_values):
    count, width = memory.shape
    block = 1024 if count % 1024 == 0 else count
    row_spec = pl.BlockSpec((block, width), lambda i, *_: (i, 0))
    half = fixed((2, width // 2, width))
    return call(
        memory_pull_body,
        "memory_backward",
        (count // block,),
        [row_spec, fixed((1, width)), fixed(cross_key.shape), fixed(cross_value.shape), row_spec, row_spec],
        [row_spec, half, half],
        [shaped((count, width), BF16)] + [shaped((2, width // 2, width), BF16)] * 2,
        [pltpu.VMEM((width, width), F32)] * 2 + [pltpu.VMEM((width, width), BF16)],
        prefetch=1,
    )(codes, memory, encoder_gain, cross_key, cross_value, grad_keys, grad_values)


def causal_bias():
    key_at = lax.broadcasted_iota(jnp.int32, (SEQ, 2 * SEQ), 0)
    query_at = lax.broadcasted_iota(jnp.int32, (SEQ, 2 * SEQ), 1) % SEQ
    return jnp.where(key_at <= query_at, 0.0, MASKED).astype(F32)


def softmax_columns(scores):
    largest = jnp.max(scores, axis=0, keepdims=True)
    powered = jnp.exp(scores - largest)
    inverse = 1.0 / jnp.sum(powered, axis=0, keepdims=True)
    return powered.astype(BF16), inverse


def self_body(
    per_step, input_ref, self_gain_ref, cross_gain_ref, query_ref, key_ref, value_ref, output_ref, cross_ref,
    queries_ref, keys_ref, values_ref, powered_ref, inverse_ref, blend_ref, attended_ref, after_ref, cross_queries_ref,
):
    rows = input_ref[...].astype(F32)
    normed = (rows * inverse_rms(rows) * self_gain_ref[...]).astype(BF16)
    queries = dot_nn(normed, query_ref[...]).astype(BF16)
    keys = dot_nn(normed, key_ref[...]).astype(BF16)
    values = dot_nn(normed, value_ref[...]).astype(BF16)
    queries_ref[...] = queries
    keys_ref[...] = keys
    values_ref[...] = values
    bias = causal_bias()
    for member in range(per_step):
        tokens = slice(member * SEQ, (member + 1) * SEQ)
        for pair in range(PAIRS):
            lanes = slice(pair * PAIR, (pair + 1) * PAIR)
            columns = slice(pair * 2 * SEQ, (pair + 1) * 2 * SEQ)
            scores = dot_nt(keys[tokens, lanes], head_pair_rows(queries[tokens, lanes])) + bias
            powered, inverse = softmax_columns(scores)
            powered_ref[member, :, columns] = powered
            inverse_ref[member, :, columns] = inverse
            blend = head_pair_diagonal(dot_tn(values[tokens, lanes], powered) * inverse, SEQ)
            blend_ref[member, lanes, :] = blend.astype(BF16)
            attended_ref[tokens, lanes] = blend.T.astype(BF16)
    after = rows + dot_nn(attended_ref[...], output_ref[...])
    after_ref[...] = after
    cross_normed = (after * inverse_rms(after) * cross_gain_ref[...]).astype(BF16)
    cross_queries_ref[...] = dot_nn(cross_normed, cross_ref[...]).astype(BF16)


def self_forward(inputs, self_gain, cross_gain, self_query, self_key, self_value, self_output, cross_query):
    tokens, width = inputs.shape
    queries_here = tokens // SEQ
    per_step = 2 if queries_here % 2 == 0 else 1
    block = per_step * SEQ
    row_spec = pl.BlockSpec((block, width), lambda i: (i, 0))
    weight = fixed((width, width))
    columns = HEADS * SEQ

    def query_spec(*shape):
        return pl.BlockSpec((per_step,) + shape, lambda i: (i, 0, 0))

    return call(
        functools.partial(self_body, per_step),
        "self_forward",
        (queries_here // per_step,),
        [row_spec, fixed((1, width)), fixed((1, width))] + [weight] * 5,
        [
            row_spec, row_spec, row_spec,
            query_spec(SEQ, columns), query_spec(1, columns), query_spec(width, SEQ),
            row_spec, row_spec, row_spec,
        ],
        [
            shaped((tokens, width), BF16), shaped((tokens, width), BF16), shaped((tokens, width), BF16),
            shaped((queries_here, SEQ, columns), BF16),
            shaped((queries_here, 1, columns), F32),
            shaped((queries_here, width, SEQ), BF16),
            shaped((tokens, width), BF16), shaped((tokens, width), F32), shaped((tokens, width), BF16),
        ],
    )(inputs, self_gain, cross_gain, self_query, self_key, self_value, self_output, cross_query)


def self_pull_body(
    per_step, codes_ref, grad_ref, queries_ref, keys_ref, values_ref, powered_ref, inverse_ref, blend_ref, output_ref,
    input_ref, grad_all_ref, gain_ref, query_ref, key_ref, value_ref,
    grad_inputs_ref, keep_a_ref, send_a_ref, keep_b_ref, send_b_ref,
    pull_queries, pull_keys, pull_values, staged,
):
    step = pl.program_id(0)
    block = per_step * SEQ
    here = pl.ds(pl.multiple_of(step * block, block), block)
    grad_attended = dot_nt(grad_ref[...].astype(BF16), output_ref[...]).astype(BF16)
    made_queries, made_keys, made_values = [], [], []
    for member in range(per_step):
        tokens = slice(member * SEQ, (member + 1) * SEQ)
        for pair in range(PAIRS):
            lanes = slice(pair * PAIR, (pair + 1) * PAIR)
            columns = slice(pair * 2 * SEQ, (pair + 1) * 2 * SEQ)
            inverse = inverse_ref[member, :, columns]
            scale = jnp.concatenate(
                [
                    jnp.broadcast_to(inverse[:, :SEQ], (HDIM, SEQ)),
                    jnp.broadcast_to(inverse[:, SEQ:], (HDIM, SEQ)),
                ],
                axis=0,
            )
            turned = grad_attended[tokens, lanes].astype(F32).T * scale
            inner = turned * blend_ref[member, lanes, :].astype(F32)
            inner_sum = jnp.concatenate(
                [
                    jnp.sum(inner[:HDIM], axis=0, keepdims=True),
                    jnp.sum(inner[HDIM:], axis=0, keepdims=True),
                ],
                axis=1,
            )
            grad_rows = head_pair_rows(turned.T.astype(BF16))
            powered = powered_ref[member, :, columns]
            grad_powered = dot_nt(values_ref[tokens, lanes], grad_rows)
            grad_scores = (powered.astype(F32) * (grad_powered - inner_sum)).astype(BF16)
            made_values.append(dot_nn(powered, grad_rows))
            made_keys.append(dot_nn(grad_scores, head_pair_rows(queries_ref[tokens, lanes])))
            made_queries.append(head_pair_diagonal(dot_tn(keys_ref[tokens, lanes], grad_scores), SEQ).T)

    def assemble(pieces):
        return jnp.concatenate(
            [
                jnp.concatenate(pieces[member * PAIRS : (member + 1) * PAIRS], axis=1)
                for member in range(per_step)
            ],
            axis=0,
        ).astype(BF16)

    pull_queries[here, :] = assemble(made_queries)
    pull_keys[here, :] = assemble(made_keys)
    pull_values[here, :] = assemble(made_values)

    @pl.when(step == pl.num_programs(0) - 1)
    def _():
        rows = input_ref[...].astype(F32)
        scale = inverse_rms(rows)
        normed = (rows * scale * gain_ref[...]).astype(BF16)
        queries, keys, values = pull_queries[...], pull_keys[...], pull_values[...]
        store_turned(codes_ref[0], dot_tn(normed, queries), keep_a_ref, send_a_ref, 0, staged)
        store_turned(codes_ref[0], dot_tn(normed, keys), keep_a_ref, send_a_ref, 1, staged)
        store_turned(codes_ref[1], dot_tn(normed, values), keep_b_ref, send_b_ref, 0, staged)
        grad_normed = (
            dot_nt(queries, query_ref[...]) + dot_nt(keys, key_ref[...]) + dot_nt(values, value_ref[...])
        )
        grad_inputs_ref[...] = grad_all_ref[...] + norm_pull(rows, scale, gain_ref[...], grad_normed)


def self_backward(
    codes, grad_after, queries, keys, values, powered, inverse, blend, self_output, inputs, self_gain, self_query, self_key, self_value
):
    tokens, width = inputs.shape
    queries_here = tokens // SEQ
    per_step = 2 if queries_here % 2 == 0 else 1
    block = per_step * SEQ
    row_spec = pl.BlockSpec((block, width), lambda i, *_: (i, 0))
    weight = fixed((width, width))
    columns = HEADS * SEQ
    whole = fixed((tokens, width))

    def query_spec(*shape):
        return pl.BlockSpec((per_step,) + shape, lambda i, *_: (i, 0, 0))

    return call(
        functools.partial(self_pull_body, per_step),
        "self_backward",
        (queries_here // per_step,),
        [
            row_spec, row_spec, row_spec, row_spec,
            query_spec(SEQ, columns), query_spec(1, columns), query_spec(width, SEQ), weight,
            whole, whole, fixed((1, width)), weight, weight, weight,
        ],
        [whole] + [fixed((2, width // 2, width))] * 2 + [fixed((1, width // 2, width))] * 2,
        [shaped((tokens, width), F32)]
        + [shaped((2, width // 2, width), BF16)] * 2
        + [shaped((1, width // 2, width), BF16)] * 2,
        [pltpu.VMEM((tokens, width), BF16)] * 3 + [pltpu.VMEM((width, width), BF16)],
        prefetch=1,
    )(
        codes, grad_after, queries, keys, values, powered, inverse, blend, self_output,
        inputs, grad_after, self_gain, self_query, self_key, self_value,
    )


def cross_body(
    chosen_ref, queries_ref, keys_ref, values_t_ref, ids_ref, powered_ref, inverse_ref, blend_ref, attended_ref
):
    member = pl.program_id(0)
    ids = ids_ref[0]
    seen = ids == chosen_ref[member, 0]
    for place in range(1, chosen_ref.shape[1]):
        seen = seen | (ids == chosen_ref[member, place])
    bias = jnp.where(seen, 0.0, MASKED).astype(F32)
    bias = jnp.concatenate([bias, bias], axis=1)
    for pair in range(PAIRS):
        lanes = slice(pair * PAIR, (pair + 1) * PAIR)
        columns = slice(pair * 2 * SEQ, (pair + 1) * 2 * SEQ)
        scores = dot_nt(keys_ref[0, :, lanes], head_pair_rows(queries_ref[:, lanes])) + bias
        powered, inverse = softmax_columns(scores)
        powered_ref[0, :, columns] = powered
        inverse_ref[0, :, columns] = inverse
        blend = head_pair_diagonal(dot_nn(values_t_ref[0, lanes, :], powered) * inverse, SEQ)
        blend_ref[0, lanes, :] = blend.astype(BF16)
        attended_ref[:, lanes] = blend.T.astype(BF16)


def cross_forward(chosen, queries, keys, values_t, ids):
    tokens, width = queries.shape
    queries_here = tokens // SEQ
    shared = keys.shape[0] == 1
    slots = keys.shape[1]
    columns = HEADS * SEQ

    def pool_spec(*shape):
        return pl.BlockSpec((1,) + shape, (lambda i, *_: (0, 0, 0)) if shared else (lambda i, *_: (i, 0, 0)))

    def query_spec(*shape):
        return pl.BlockSpec((1,) + shape, lambda i, *_: (i, 0, 0))

    row_spec = pl.BlockSpec((SEQ, width), lambda i, *_: (i, 0))
    return call(
        cross_body,
        "cross_forward",
        (queries_here,),
        [row_spec, pool_spec(slots, width), pool_spec(width, slots), pool_spec(slots, SEQ)],
        [query_spec(slots, columns), query_spec(1, columns), query_spec(width, SEQ), row_spec],
        [
            shaped((queries_here, slots, columns), BF16),
            shaped((queries_here, 1, columns), F32),
            shaped((queries_here, width, SEQ), BF16),
            shaped((tokens, width), BF16),
        ],
        prefetch=1,
    )(chosen, queries, keys, values_t, ids)


def cross_pull_body(
    shared, codes_ref, grad_ref, queries_ref, keys_t_ref, values_ref, powered_ref, inverse_ref, blend_ref,
    after_ref, grad_cross_ref, gain_ref, query_ref, attended_ref,
    grad_keys_ref, grad_values_ref, grad_after_ref, keep_ref, send_ref,
    pull_queries, staged,
):
    step = pl.program_id(0)
    here = pl.ds(pl.multiple_of(step * SEQ, SEQ), SEQ)

    def clear():
        grad_keys_ref[...] = jnp.zeros_like(grad_keys_ref)
        grad_values_ref[...] = jnp.zeros_like(grad_values_ref)

    if shared:
        pl.when(step == 0)(clear)
    else:
        clear()
    for pair in range(PAIRS):
        lanes = slice(pair * PAIR, (pair + 1) * PAIR)
        columns = slice(pair * 2 * SEQ, (pair + 1) * 2 * SEQ)
        inverse = inverse_ref[0, :, columns]
        scale = jnp.concatenate(
            [
                jnp.broadcast_to(inverse[:, :SEQ], (HDIM, SEQ)),
                jnp.broadcast_to(inverse[:, SEQ:], (HDIM, SEQ)),
            ],
            axis=0,
        )
        turned = grad_ref[:, lanes].astype(F32).T * scale
        inner = turned * blend_ref[0, lanes, :].astype(F32)
        inner_sum = jnp.concatenate(
            [
                jnp.sum(inner[:HDIM], axis=0, keepdims=True),
                jnp.sum(inner[HDIM:], axis=0, keepdims=True),
            ],
            axis=1,
        )
        grad_rows = head_pair_rows(turned.T.astype(BF16))
        powered = powered_ref[0, :, columns]
        grad_powered = dot_nt(values_ref[0, :, lanes], grad_rows)
        grad_scores = (powered.astype(F32) * (grad_powered - inner_sum)).astype(BF16)
        grad_values_ref[0, :, lanes] += dot_nn(powered, grad_rows)
        grad_keys_ref[0, :, lanes] += dot_nn(grad_scores, head_pair_rows(queries_ref[:, lanes]))
        pulled = head_pair_diagonal(dot_nn(keys_t_ref[0, lanes, :], grad_scores), SEQ)
        pull_queries[here, lanes] = pulled.T.astype(BF16)

    @pl.when(step == pl.num_programs(0) - 1)
    def _():
        rows = after_ref[...]
        scale = inverse_rms(rows)
        normed = (rows * scale * gain_ref[...]).astype(BF16)
        pulled = pull_queries[...]
        store_turned(codes_ref[0], dot_tn(normed, pulled), keep_ref, send_ref, 0, staged)
        grad_after = grad_cross_ref[...] + norm_pull(
            rows, scale, gain_ref[...], dot_nt(pulled, query_ref[...])
        )
        grad_after_ref[...] = grad_after
        grad_output = dot_tn(attended_ref[...], grad_after.astype(BF16))
        store_turned(codes_ref[0], grad_output, keep_ref, send_ref, 1, staged)


def cross_backward(
    codes, grad_attended, queries, keys_t, values, powered, inverse, blend, after_self, grad_after_cross, cross_gain, cross_query, self_attended
):
    tokens, width = queries.shape
    queries_here = tokens // SEQ
    shared = values.shape[0] == 1
    pools, slots = values.shape[:2]
    columns = HEADS * SEQ
    weight = fixed((width, width))
    whole = fixed((tokens, width))

    def pool_spec(*shape):
        return pl.BlockSpec((1,) + shape, (lambda i, *_: (0, 0, 0)) if shared else (lambda i, *_: (i, 0, 0)))

    def query_spec(*shape):
        return pl.BlockSpec((1,) + shape, lambda i, *_: (i, 0, 0))

    row_spec = pl.BlockSpec((SEQ, width), lambda i, *_: (i, 0))
    half = fixed((2, width // 2, width))
    return call(
        functools.partial(cross_pull_body, shared),
        "cross_backward",
        (queries_here,),
        [
            row_spec, row_spec, pool_spec(width, slots), pool_spec(slots, width),
            query_spec(slots, columns), query_spec(1, columns), query_spec(width, SEQ),
            whole, whole, fixed((1, width)), weight, whole,
        ],
        [pool_spec(slots, width), pool_spec(slots, width), whole, half, half],
        [
            shaped((pools, slots, width), F32), shaped((pools, slots, width), F32),
            shaped((tokens, width), F32),
            shaped((2, width // 2, width), BF16), shaped((2, width // 2, width), BF16),
        ],
        [pltpu.VMEM((tokens, width), BF16), pltpu.VMEM((width, width), BF16)],
        prefetch=1,
    )(
        codes, grad_attended, queries, keys_t, values, powered, inverse, blend,
        after_self, grad_after_cross, cross_gain, cross_query, self_attended,
    )


TANH_SLOPE = 0.7978845608028654
TANH_CUBE = 0.044715


def feed_body(
    limits_ref, codes_ref, after_ref, attended_ref, cotangent_ref, gain_ref, output_ref, inner_ref, outer_ref,
    layer_ref, grad_after_ref, grad_attended_ref, keep_a_ref, send_a_ref, keep_b_ref, send_b_ref, keep_c_ref, send_c_ref,
    after_cross, normed, grad_feed, total, grad_normed, staged,
):
    step = pl.program_id(0)
    tokens = after_cross.shape[0]

    @pl.when(step == 0)
    def _():
        rows = after_ref[...] + dot_nn(attended_ref[...], output_ref[...])
        after_cross[...] = rows
        total[...] = rows
        normed[...] = (rows * inverse_rms(rows) * gain_ref[...]).astype(BF16)
        grad_normed[...] = jnp.zeros_like(grad_normed)
        place = lax.broadcasted_iota(jnp.int32, (SEQ, cotangent_ref.shape[1]), 0)
        for member in range(tokens // SEQ):
            span = slice(member * SEQ, (member + 1) * SEQ)
            grads = cotangent_ref[span, :]
            grad_feed[span, :] = jnp.where(place < limits_ref[member], grads, jnp.zeros_like(grads))

    inner = inner_ref[...]
    outer = outer_ref[...]
    grads = grad_feed[...]
    pre = dot_nn(normed[...], inner)
    squared = pre * pre
    half = 0.5 * jnp.tanh(pre * (TANH_SLOPE + (TANH_SLOPE * TANH_CUBE) * squared)) + 0.5
    hidden = (pre * half).astype(BF16)
    slope = half + (pre * (2.0 * half * (1.0 - half))) * (
        TANH_SLOPE + (3.0 * TANH_SLOPE * TANH_CUBE) * squared
    )
    total[...] += dot_nn(hidden, outer)
    grad_pre = (dot_nt(grads, outer) * slope).astype(BF16)
    store_turned(codes_ref[0], dot_tn(hidden, grads), keep_a_ref, send_a_ref, 0, staged)
    store_turned(codes_ref[1], dot_tn(normed[...], grad_pre), keep_b_ref, send_b_ref, 0, staged)
    grad_normed[...] += dot_nt(grad_pre, inner)

    @pl.when(step == pl.num_programs(0) - 1)
    def _():
        layer_ref[...] = total[...].astype(BF16)
        rows = after_cross[...]
        scale = inverse_rms(rows)
        grad_rows = norm_pull(rows, scale, gain_ref[...], grad_normed[...])
        grad_after = grad_feed[...].astype(F32) + grad_rows
        grad_after_ref[...] = grad_after
        branch = grad_after.astype(BF16)
        store_turned(codes_ref[0], dot_tn(attended_ref[...], branch), keep_c_ref, send_c_ref, 0, staged)
        grad_attended_ref[...] = dot_nt(branch, output_ref[...]).astype(BF16)


def feed_both(limits, codes, after_self, attended, cotangent, feed_gain, cross_output, inner_weight, outer_weight):
    tokens, width = after_self.shape
    hidden = inner_weight.shape[1]
    block = width
    steps = hidden // block
    whole = fixed((tokens, width))
    weight = fixed((width, width))
    inner_spec = pl.BlockSpec((width, block), lambda i, *_: (0, i))
    outer_spec = pl.BlockSpec((block, width), lambda i, *_: (i, 0))
    half_spec = pl.BlockSpec((1, width // 2, width), lambda i, *_: (i, 0, 0))
    return call(
        feed_body,
        "feed_both",
        (steps,),
        [whole, whole, whole, fixed((1, width)), weight, inner_spec, outer_spec],
        [whole, whole, whole] + [half_spec] * 4 + [fixed((1, width // 2, width))] * 2,
        [shaped((tokens, width), BF16), shaped((tokens, width), F32), shaped((tokens, width), BF16)]
        + [shaped((steps, width // 2, width), BF16)] * 4
        + [shaped((1, width // 2, width), BF16)] * 2,
        [
            pltpu.VMEM((tokens, width), F32), pltpu.VMEM((tokens, width), BF16), pltpu.VMEM((tokens, width), BF16),
            pltpu.VMEM((tokens, width), F32), pltpu.VMEM((tokens, width), F32),
            pltpu.VMEM((width, width), BF16),
        ],
        prefetch=2,
    )(limits, codes, after_self, attended, cotangent, feed_gain, cross_output, inner_weight, outer_weight)


def permute(values, batch_bits, mem_bits):
    if batch_bits:
        axis, bits, count = "batch", batch_bits, lax.axis_size("batch")
    else:
        axis, bits, count = "mem", mem_bits, lax.axis_size("mem")
    return lax.ppermute(values, axis, [(at, at ^ bits) for at in range(count)])


CORE, ACROSS, ALONG = (1, 0), (2, 0), (0, 1)
DEEP = ((0, 2), (0, 4), (0, 6))


def added(*terms):
    total = terms[0].astype(F32)
    for term in terms[1:]:
        total = total + term.astype(F32)
    return total.astype(BF16)


def portions(count, *terms):
    size = terms[0].shape[1] // count
    return [added(*[t[:, i * size : (i + 1) * size] for t in terms]) for i in range(count)]


def beyond(values):
    bits = 8
    while bits < lax.axis_size("mem"):
        values = added(values, permute(values, 0, bits))
        bits *= 2
    return values


def reduce_all(keep_a, send_a, keep_b, send_b):
    count = keep_a.shape[0]
    got_a, got_b = permute(send_a, *CORE), permute(send_b, *CORE)
    keep_a, send_a = portions(2, keep_a, got_a)
    keep_b, send_b = portions(2, keep_b, got_b)
    got_a, got_b = permute(send_a, *ACROSS), permute(send_b, *ALONG)
    keep_a, send_a = portions(2, keep_a, got_a)
    keep_b, send_b = portions(2, keep_b, got_b)
    got_a, got_b = permute(send_a, *ALONG), permute(send_b, *ACROSS)
    parts_a = portions(4, keep_a, got_a)
    parts_b = portions(4, keep_b, got_b)
    parts = [jnp.concatenate([a, b], axis=0) for a, b in zip(parts_a, parts_b)]
    own = beyond(added(parts[0], *[permute(p, *bits) for p, bits in zip(parts[1:], DEEP)]))
    whole = jnp.concatenate([own] + [permute(own, *bits) for bits in DEEP], axis=1)
    whole_a, whole_b = whole[:count], whole[count:]
    got_a, got_b = permute(whole_a, *ALONG), permute(whole_b, *ACROSS)
    whole_a = jnp.concatenate([whole_a, got_a], axis=1)
    whole_b = jnp.concatenate([whole_b, got_b], axis=1)
    got_a, got_b = permute(whole_a, *ACROSS), permute(whole_b, *ALONG)
    whole_a = jnp.concatenate([whole_a, got_a], axis=1)
    whole_b = jnp.concatenate([whole_b, got_b], axis=1)
    return whole_a, permute(whole_a, *CORE), whole_b, permute(whole_b, *CORE)


def restore(code, own, other, at, target, rows):
    size = 2 * own.shape[1] // BLOCKS
    half = BLOCKS // 2
    for place in range(BLOCKS):
        source = own if place < half else other
        start = (place % half) * size
        goal = pl.ds(pl.multiple_of((place ^ code) * size + rows, size), size)
        target[goal, :] = source[at, start : start + size, :].astype(F32)


def fold_lanes(values):
    total = values[:, :128]
    for start in range(128, values.shape[1], 128):
        total = total + values[:, start : start + 128]
    return total


def restore_stack_body(codes_ref, own_ref, other_ref, out_ref):
    restore(codes_ref[0], own_ref, other_ref, 0, out_ref, 0)


def restore_rows(codes, own, other):
    count, half, width = own.shape
    spec = pl.BlockSpec((1, half, width), lambda i, *_: (i, 0, 0))
    return call(
        restore_stack_body, "restore_rows", (count,), [spec, spec],
        pl.BlockSpec((2 * half, width), lambda i, *_: (i, 0)),
        shaped((count * 2 * half, width), F32), prefetch=1,
    )(codes, own, other)


def restore_columns_body(codes_ref, own_ref, other_ref, weight_ref, gain_ref, out_ref, grad_gain_ref, sums):
    step = pl.program_id(0)

    @pl.when(step == 0)
    def _():
        sums[...] = jnp.zeros_like(sums)

    restore(codes_ref[1], own_ref, other_ref, 0, out_ref, 0)
    sums[...] += fold_lanes(out_ref[...] * weight_ref[...].astype(F32))

    @pl.when(step == pl.num_programs(0) - 1)
    def _():
        grad_gain_ref[...] = jnp.sum(sums[...].T, axis=0, keepdims=True) / gain_ref[...]


def restore_columns(codes, own, other, weight, gain):
    count, half, width = own.shape
    spec = pl.BlockSpec((1, half, width), lambda i, *_: (i, 0, 0))
    wide = pl.BlockSpec((2 * half, width), lambda i, *_: (0, i))
    return call(
        restore_columns_body, "restore_columns", (count,), [spec, spec, wide, fixed((1, 2 * half))],
        [wide, fixed((1, 2 * half))],
        [shaped((2 * half, count * width), F32), shaped((1, 2 * half), F32)],
        [pltpu.VMEM((2 * half, 128), F32)], prefetch=1,
    )(codes, own, other, weight, gain)


def restore_cross_body(
    codes_ref, own_a_ref, other_a_ref, own_b_ref, other_b_ref, query_ref, key_ref, value_ref, cross_gain_ref, encoder_gain_ref,
    output_out, query_out, self_out, key_out, value_out, cross_gain_out, encoder_gain_out,
):
    restore(codes_ref[0], own_a_ref, other_a_ref, 0, output_out, 0)
    restore(codes_ref[0], own_a_ref, other_a_ref, 1, query_out, 0)
    restore(codes_ref[0], own_a_ref, other_a_ref, 2, self_out, 0)
    restore(codes_ref[1], own_b_ref, other_b_ref, 0, key_out, 0)
    restore(codes_ref[1], own_b_ref, other_b_ref, 1, value_out, 0)
    sums = fold_lanes(query_out[...] * query_ref[...].astype(F32))
    cross_gain_out[...] = jnp.sum(sums.T, axis=0, keepdims=True) / cross_gain_ref[...]
    sums = fold_lanes(
        key_out[...] * key_ref[...].astype(F32) + value_out[...] * value_ref[...].astype(F32)
    )
    encoder_gain_out[...] = jnp.sum(sums.T, axis=0, keepdims=True) / encoder_gain_ref[...]


def restore_cross(codes, own_a, other_a, own_b, other_b, cross_query, cross_key, cross_value, cross_gain, encoder_gain):
    width = own_a.shape[2]
    weight, row = fixed((width, width)), fixed((1, width))
    return call(
        restore_cross_body, "restore_cross", (1,),
        [fixed(own_a.shape)] * 2 + [fixed(own_b.shape)] * 2 + [weight] * 3 + [row] * 2,
        [weight] * 5 + [row] * 2,
        [shaped((width, width), F32)] * 5 + [shaped((1, width), F32)] * 2, prefetch=1,
    )(codes, own_a, other_a, own_b, other_b, cross_query, cross_key, cross_value, cross_gain, encoder_gain)


def restore_self_body(
    codes_ref, own_a_ref, other_a_ref, own_b_ref, other_b_ref, query_ref, key_ref, value_ref, gain_ref,
    query_out, key_out, value_out, gain_out,
):
    restore(codes_ref[0], own_a_ref, other_a_ref, 0, query_out, 0)
    restore(codes_ref[0], own_a_ref, other_a_ref, 1, key_out, 0)
    restore(codes_ref[1], own_b_ref, other_b_ref, 0, value_out, 0)
    sums = fold_lanes(
        query_out[...] * query_ref[...].astype(F32)
        + key_out[...] * key_ref[...].astype(F32)
        + value_out[...] * value_ref[...].astype(F32)
    )
    gain_out[...] = jnp.sum(sums.T, axis=0, keepdims=True) / gain_ref[...]


def restore_self(codes, own_a, other_a, own_b, other_b, self_query, self_key, self_value, self_gain):
    width = own_a.shape[2]
    weight, row = fixed((width, width)), fixed((1, width))
    return call(
        restore_self_body, "restore_self", (1,),
        [fixed(own_a.shape)] * 2 + [fixed(own_b.shape)] * 2 + [weight] * 3 + [row],
        [weight] * 3 + [row],
        [shaped((width, width), F32)] * 3 + [shaped((1, width), F32)], prefetch=1,
    )(codes, own_a, other_a, own_b, other_b, self_query, self_key, self_value, self_gain)


def device_codes():
    batch_at, mem_at = lax.axis_index("batch"), lax.axis_index("mem")
    core, across = batch_at & 1, batch_at >> 1
    along, deep = mem_at & 1, (mem_at >> 1) & 3
    return jnp.stack(
        [
            (core << 4) | (across << 3) | (along << 2) | deep,
            (core << 4) | (along << 3) | (across << 2) | deep,
        ]
    ).astype(jnp.int32)


def passage_slots(pool_ids, chosen, passages, pool_rows):
    passage_marks = jnp.arange(passages, dtype=jnp.int32)
    starts = jnp.sum(
        (pool_ids[None, :] < passage_marks[:, None]).astype(jnp.int32), axis=1, dtype=jnp.int32
    )
    counts = jnp.sum(
        (pool_ids[None, :] == passage_marks[:, None]).astype(jnp.int32), axis=1, dtype=jnp.int32
    )
    picked = (chosen[..., None] == passage_marks).astype(jnp.int32)
    first_row = jnp.sum(picked * starts, axis=-1, dtype=jnp.int32)
    extent = jnp.sum(picked * counts, axis=-1, dtype=jnp.int32)
    offsets = jnp.arange(PLEN, dtype=jnp.int32)
    slot_rows = jnp.minimum(first_row[..., None] + offsets, pool_rows - 1)
    slot_visible = offsets < extent[..., None]
    slot_shape = (chosen.shape[0], chosen.shape[1] * PLEN)
    return (slot_rows.reshape(slot_shape), slot_visible.reshape(slot_shape))


def local(
    inputs,
    cotangent,
    memory,
    passage_ids,
    retrieved,
    task_ids,
    target_lens,
    encoder_gain,
    self_gain,
    cross_gain,
    feed_gain,
    self_query,
    self_key,
    self_value,
    self_output,
    cross_query,
    cross_key,
    cross_value,
    cross_output,
    inner_weight,
    outer_weight,
):
    width = inputs.shape[2]
    own_rows = memory.shape[1]
    chosen = retrieved[0]
    codes = device_codes()
    encoder_row, self_row, cross_row, feed_row = (
        member.reshape(1, width) for member in (encoder_gain, self_gain, cross_gain, feed_gain)
    )
    pool_memory = lax.all_gather(memory[0], "mem", axis=0, tiled=True)
    pool_ids = lax.all_gather(passage_ids[0], "mem", axis=0, tiled=True)
    pool_rows = pool_memory.shape[0]
    (
        self_queries, self_keys, self_values, self_powered, self_inverse, self_blend,
        self_attended, after_self, cross_queries,
    ) = self_forward(
        inputs[0], self_row, cross_row, self_query, self_key, self_value, self_output, cross_query
    )
    pool_keys, pool_values, pool_keys_t, pool_values_t = memory_forward(
        pool_memory, encoder_row, cross_key, cross_value
    )
    slots = chosen.shape[1] * PLEN
    shared = pool_rows <= slots
    if shared:
        keys, values = pool_keys[None], pool_values[None]
        keys_t, values_t = pool_keys_t[None], pool_values_t[None]
        ids = pool_ids[None]
    else:
        passages = PASS_DEV * lax.axis_size("mem")
        slot_rows, slot_visible = passage_slots(pool_ids, chosen, passages, pool_rows)
        keys = jnp.take(pool_keys, slot_rows, axis=0)
        values = jnp.take(pool_values, slot_rows, axis=0)
        keys_t, values_t = jnp.swapaxes(keys, 1, 2), jnp.swapaxes(values, 1, 2)
        ids = jnp.where(slot_visible, jnp.take(pool_ids, slot_rows), -1)
    ids = jnp.broadcast_to(ids[..., None], ids.shape + (SEQ,))
    cross_powered, cross_inverse, cross_blend, cross_attended = cross_forward(
        chosen, cross_queries, keys, values_t, ids
    )
    limits = jnp.minimum(target_lens[0], SEQ - task_ids[0] * (SEQ // 4))
    (
        layer_out, grad_after_cross, grad_cross_attended, outer_keep, outer_send, inner_keep, inner_send,
        output_keep, output_send,
    ) = feed_both(
        limits, codes, after_self, cross_attended, cotangent[0], feed_row, cross_output, inner_weight, outer_weight
    )
    feed_sums = reduce_all(outer_keep, outer_send, inner_keep, inner_send)
    grad_keys, grad_values, grad_after_self, query_keep, query_send = cross_backward(
        codes, grad_cross_attended, cross_queries, keys_t, values, cross_powered, cross_inverse, cross_blend,
        after_self, grad_after_cross, cross_row, cross_query, self_attended,
    )
    if shared:
        pool_grad_keys, pool_grad_values = grad_keys[0], grad_values[0]
    else:
        slot_index = jnp.where(slot_visible, slot_rows, pool_rows).reshape(-1)
        empty = jnp.zeros((pool_rows, width), F32)
        pool_grad_keys = empty.at[slot_index].add(grad_keys.reshape(-1, width), mode="drop")
        pool_grad_values = empty.at[slot_index].add(grad_values.reshape(-1, width), mode="drop")
    grad_pool_normed, pool_keep, pool_send = memory_backward(
        codes, pool_memory, encoder_row, cross_key, cross_value, pool_grad_keys, pool_grad_values
    )
    grad_own_normed = lax.psum_scatter(grad_pool_normed, "mem", scatter_dimension=0, tiled=True)
    memory_rows = memory[0].astype(F32)
    grad_memory = norm_pull(
        memory_rows, inverse_rms(memory_rows), encoder_row, grad_own_normed.astype(F32)
    )
    cross_sums = reduce_all(
        jnp.concatenate([output_keep, query_keep], axis=0),
        jnp.concatenate([output_send, query_send], axis=0),
        pool_keep,
        pool_send,
    )
    grad_inputs, self_keep_a, self_send_a, self_keep_b, self_send_b = self_backward(
        codes, grad_after_self, self_queries, self_keys, self_values, self_powered, self_inverse, self_blend,
        self_output, inputs[0], self_row, self_query, self_key, self_value,
    )
    self_sums = reduce_all(self_keep_a, self_send_a, self_keep_b, self_send_b)
    grad_outer = restore_rows(codes, feed_sums[0], feed_sums[1])
    grad_inner, grad_feed_gain = restore_columns(codes, feed_sums[2], feed_sums[3], inner_weight, feed_row)
    (
        grad_cross_output, grad_cross_query, grad_self_output, grad_cross_key, grad_cross_value,
        grad_cross_gain, grad_encoder_gain,
    ) = restore_cross(
        codes, *cross_sums, cross_query, cross_key, cross_value, cross_row, encoder_row
    )
    grad_self_query, grad_self_key, grad_self_value, grad_self_gain = restore_self(
        codes, *self_sums, self_query, self_key, self_value, self_row
    )
    return (
        layer_out[None],
        grad_inputs[None],
        grad_memory[None],
        grad_encoder_gain[0],
        grad_self_gain[0],
        grad_cross_gain[0],
        grad_feed_gain[0],
        grad_self_query,
        grad_self_key,
        grad_self_value,
        grad_self_output,
        grad_cross_query,
        grad_cross_key,
        grad_cross_value,
        grad_cross_output,
        grad_inner,
        grad_outer,
    )


def solution(mesh):
    spread = (P("batch", "mem", None),) * 3
    in_specs = spread + (
        P("batch", "mem"), P("batch", "mem", None), P("batch", "mem"), P("batch", "mem"),
    ) + (P(),) * 14
    out_specs = spread + (P(),) * 14
    return jax.shard_map(local, mesh=mesh, in_specs=in_specs, out_specs=out_specs, check_vma=False)
```

```python
import functools

import jax
import jax.numpy as jnp
from jax import lax
from jax.experimental import pallas as pl
from jax.experimental.pallas import tpu as pltpu
from jax.sharding import PartitionSpec as P

HEADS = 8
HDIM = 64
SEQ = 128
PLEN = 256
PASS_DEV = 1
PAIRS = HEADS // 2
PAIR = 2 * HDIM

EPSILON = 1e-06
MASKED = -1e30
F32 = jnp.float32
BF16 = jnp.bfloat16
MIB = 1024 * 1024
BLOCKS = 32


def dot_nn(former, latter):
    return lax.dot_general(
        former, latter, (((1,), (0,)), ((), ())), preferred_element_type=F32
    )


def dot_tn(former, latter):
    return lax.dot_general(
        former, latter, (((0,), (0,)), ((), ())), preferred_element_type=F32
    )


def dot_nt(former, latter):
    return lax.dot_general(
        former, latter, (((1,), (1,)), ((), ())), preferred_element_type=F32
    )


def inverse_rms(values):
    return lax.rsqrt(jnp.mean(values * values, axis=-1, keepdims=True) + EPSILON)


def norm_pull(values, row_scale, norm_gain, grad_normed):
    weighted = grad_normed * norm_gain
    cubed = row_scale * row_scale * row_scale
    grad_values = row_scale * weighted - values * (
        cubed * jnp.mean(values * weighted, axis=-1, keepdims=True)
    )
    return grad_values


def head_pair_rows(values):
    lane = lax.broadcasted_iota(jnp.int32, values.shape, 1)
    zero = jnp.zeros_like(values)
    return jnp.concatenate(
        [jnp.where(lane < HDIM, values, zero), jnp.where(lane < HDIM, zero, values)], axis=0
    )


def head_pair_diagonal(values, rows):
    return jnp.concatenate([values[:HDIM, :rows], values[HDIM:, rows:]], axis=0)


def store_turned(code, value, keep_ref, send_ref, at, staged):
    staged[...] = value.astype(BF16)
    blocks = BLOCKS
    size = value.shape[0] // blocks
    for place in range(blocks):
        source = pl.ds(pl.multiple_of((place ^ code) * size, size), size)
        half = blocks // 2
        target = keep_ref if place < half else send_ref
        start = (place % half) * size
        target[at, start : start + size, :] = staged[source, :]


def call(body, name, grid, in_specs, out_specs, out_shape, scratch=(), prefetch=0, vmem=56, cost=5, after=()):
    first = prefetch + len(in_specs)

    def waiting(*refs):
        body(*refs[:first], *refs[first + len(after) :])

    kernel = pl.pallas_call(
        waiting,
        name=name,
        grid_spec=pltpu.PrefetchScalarGridSpec(
            num_scalar_prefetch=prefetch,
            grid=grid,
            in_specs=list(in_specs) + [pl.BlockSpec(memory_space=pl.ANY)] * len(after),
            out_specs=out_specs,
            scratch_shapes=list(scratch),
        ),
        out_shape=out_shape,
        cost_estimate=pl.CostEstimate(flops=int(cost * 1.15e9), bytes_accessed=0, transcendentals=0),
        compiler_params=pltpu.CompilerParams(
            vmem_limit_bytes=vmem * MIB,
            dimension_semantics=("arbitrary",) * len(grid),
        ),
    )
    return lambda *operands: kernel(*operands, *after)


def fixed(shape):
    return pl.BlockSpec(shape, lambda *_: (0,) * len(shape), pipeline_mode=pl.Buffered(1))


def shaped(shape, dtype):
    return jax.ShapeDtypeStruct(shape, dtype)


def memory_body(memory_ref, gain_ref, key_ref, value_ref, keys_ref, values_ref, keys_t_ref, values_t_ref):
    rows = memory_ref[...].astype(F32)
    normed = (rows * inverse_rms(rows) * gain_ref[...]).astype(BF16)
    keys_ref[...] = dot_nn(normed, key_ref[...]).astype(BF16)
    values_ref[...] = dot_nn(normed, value_ref[...]).astype(BF16)
    keys_t_ref[...] = lax.dot_general(
        key_ref[...], normed, (((0,), (1,)), ((), ())), preferred_element_type=F32
    ).astype(BF16)
    values_t_ref[...] = lax.dot_general(
        value_ref[...], normed, (((0,), (1,)), ((), ())), preferred_element_type=F32
    ).astype(BF16)


def memory_forward(memory, encoder_gain, cross_key, cross_value):
    count, width = memory.shape
    block = 512 if count % 512 == 0 else count
    row_spec = pl.BlockSpec((block, width), lambda i: (i, 0))
    column_spec = pl.BlockSpec((width, block), lambda i: (0, i))
    return functools.partial(call, cost=5)(
        memory_body,
        "memory_forward",
        (count // block,),
        [row_spec, fixed((1, width)), fixed(cross_key.shape), fixed(cross_value.shape)],
        [row_spec, row_spec, column_spec, column_spec],
        [shaped((count, width), BF16)] * 2 + [shaped((width, count), BF16)] * 2,
    )(memory, encoder_gain, cross_key, cross_value)


def memory_pull_body(
    codes_ref, memory_ref, gain_ref, key_ref, value_ref, keys_0, keys_1, keys_2, keys_3, values_0, values_1, values_2, values_3,
    grad_normed_ref, keep_ref, send_ref, grad_key, grad_value, staged,
):
    rows = memory_ref[...].astype(F32)
    normed = (rows * inverse_rms(rows) * gain_ref[...]).astype(BF16)
    grad_keys = jnp.concatenate([keys_0[...], keys_1[...], keys_2[...], keys_3[...]], axis=1).astype(BF16)
    grad_values = jnp.concatenate([values_0[...], values_1[...], values_2[...], values_3[...]], axis=1).astype(BF16)
    grad_normed = dot_nt(grad_keys, key_ref[...]) + dot_nt(grad_values, value_ref[...])
    grad_normed_ref[...] = grad_normed.astype(BF16)

    @pl.when(pl.program_id(0) == 0)
    def _():
        grad_key[...] = jnp.zeros_like(grad_key)
        grad_value[...] = jnp.zeros_like(grad_value)

    grad_key[...] += dot_tn(normed, grad_keys)
    grad_value[...] += dot_tn(normed, grad_values)

    @pl.when(pl.program_id(0) == pl.num_programs(0) - 1)
    def _():
        store_turned(codes_ref[1], grad_key[...], keep_ref, send_ref, 0, staged)
        store_turned(codes_ref[1], grad_value[...], keep_ref, send_ref, 1, staged)


def memory_backward(codes, memory, encoder_gain, cross_key, cross_value, grad_keys, grad_values, after):
    count, width = memory.shape
    block = 1024 if count % 1024 == 0 else count
    row_spec = pl.BlockSpec((block, width), lambda i, *_: (i, 0))
    half = fixed((2, width // 2, width))
    return functools.partial(call, cost=7)(
        memory_pull_body,
        "memory_backward",
        (count // block,),
        [row_spec, fixed((1, width)), fixed(cross_key.shape), fixed(cross_value.shape)] + [pl.BlockSpec((block, PAIR), lambda i, *_: (i, 0))] * 8,
        [row_spec, half, half],
        [shaped((count, width), BF16)] + [shaped((2, width // 2, width), BF16)] * 2,
        [pltpu.VMEM((width, width), F32)] * 2 + [pltpu.VMEM((width, width), BF16)],
        prefetch=1,
        after=after,
    )(codes, memory, encoder_gain, cross_key, cross_value, *grad_keys, *grad_values)


def causal_bias():
    key_at = lax.broadcasted_iota(jnp.int32, (SEQ, 2 * SEQ), 0)
    query_at = lax.broadcasted_iota(jnp.int32, (SEQ, 2 * SEQ), 1) % SEQ
    return jnp.where(key_at <= query_at, 0.0, MASKED).astype(F32)


def softmax_columns(scores):
    largest = jnp.max(scores, axis=0, keepdims=True)
    powered = jnp.exp(scores - largest)
    inverse = 1.0 / jnp.sum(powered, axis=0, keepdims=True)
    return powered.astype(BF16), inverse


def self_body(
    per_step, input_ref, self_gain_ref, cross_gain_ref, query_ref, key_ref, value_ref, output_ref, cross_ref,
    queries_ref, keys_ref, values_ref, powered_ref, inverse_ref, blend_ref, attended_ref, after_ref, cross_queries_ref,
):
    rows = input_ref[...].astype(F32)
    normed = (rows * inverse_rms(rows) * self_gain_ref[...]).astype(BF16)
    queries = dot_nn(normed, query_ref[...]).astype(BF16)
    keys = dot_nn(normed, key_ref[...]).astype(BF16)
    values = dot_nn(normed, value_ref[...]).astype(BF16)
    queries_ref[...] = queries
    keys_ref[...] = keys
    values_ref[...] = values
    bias = causal_bias()
    for member in range(per_step):
        tokens = slice(member * SEQ, (member + 1) * SEQ)
        for pair in range(PAIRS):
            lanes = slice(pair * PAIR, (pair + 1) * PAIR)
            columns = slice(pair * 2 * SEQ, (pair + 1) * 2 * SEQ)
            scores = dot_nt(keys[tokens, lanes], head_pair_rows(queries[tokens, lanes])) + bias
            powered, inverse = softmax_columns(scores)
            powered_ref[member, :, columns] = powered
            inverse_ref[member, :, columns] = inverse
            blend = head_pair_diagonal(dot_tn(values[tokens, lanes], powered) * inverse, SEQ)
            blend_ref[member, lanes, :] = blend.astype(BF16)
            attended_ref[tokens, lanes] = blend.T.astype(BF16)
    after = rows + dot_nn(attended_ref[...], output_ref[...])
    after_ref[...] = after
    cross_normed = (after * inverse_rms(after) * cross_gain_ref[...]).astype(BF16)
    cross_queries_ref[...] = dot_nn(cross_normed, cross_ref[...]).astype(BF16)


def self_forward(inputs, self_gain, cross_gain, self_query, self_key, self_value, self_output, cross_query):
    tokens, width = inputs.shape
    queries_here = tokens // SEQ
    per_step = 2 if queries_here % 2 == 0 else 1
    block = per_step * SEQ
    row_spec = pl.BlockSpec((block, width), lambda i: (i, 0))
    weight = fixed((width, width))
    columns = HEADS * SEQ

    def query_spec(*shape):
        return pl.BlockSpec((per_step,) + shape, lambda i: (i, 0, 0))

    return functools.partial(call, cost=9)(
        functools.partial(self_body, per_step),
        "self_forward",
        (queries_here // per_step,),
        [row_spec, fixed((1, width)), fixed((1, width))] + [weight] * 5,
        [
            row_spec, row_spec, row_spec,
            query_spec(SEQ, columns), query_spec(1, columns), query_spec(width, SEQ),
            row_spec, row_spec, row_spec,
        ],
        [
            shaped((tokens, width), BF16), shaped((tokens, width), BF16), shaped((tokens, width), BF16),
            shaped((queries_here, SEQ, columns), BF16),
            shaped((queries_here, 1, columns), F32),
            shaped((queries_here, width, SEQ), BF16),
            shaped((tokens, width), BF16), shaped((tokens, width), F32), shaped((tokens, width), BF16),
        ],
    )(inputs, self_gain, cross_gain, self_query, self_key, self_value, self_output, cross_query)


def self_pull_body(
    per_step, codes_ref, grad_ref, queries_ref, keys_ref, values_ref, powered_ref, inverse_ref, blend_ref, output_ref,
    input_ref, grad_all_ref, gain_ref, query_ref, key_ref, value_ref,
    grad_inputs_ref, keep_a_ref, send_a_ref, keep_b_ref, send_b_ref,
    pull_queries, pull_keys, pull_values, staged,
):
    step = pl.program_id(0)
    block = per_step * SEQ
    here = pl.ds(pl.multiple_of(step * block, block), block)
    grad_attended = dot_nt(grad_ref[...].astype(BF16), output_ref[...]).astype(BF16)
    made_queries, made_keys, made_values = [], [], []
    for member in range(per_step):
        tokens = slice(member * SEQ, (member + 1) * SEQ)
        for pair in range(PAIRS):
            lanes = slice(pair * PAIR, (pair + 1) * PAIR)
            columns = slice(pair * 2 * SEQ, (pair + 1) * 2 * SEQ)
            inverse = inverse_ref[member, :, columns]
            scale = jnp.concatenate(
                [
                    jnp.broadcast_to(inverse[:, :SEQ], (HDIM, SEQ)),
                    jnp.broadcast_to(inverse[:, SEQ:], (HDIM, SEQ)),
                ],
                axis=0,
            )
            turned = grad_attended[tokens, lanes].astype(F32).T * scale
            inner = turned * blend_ref[member, lanes, :].astype(F32)
            inner_sum = jnp.concatenate(
                [
                    jnp.sum(inner[:HDIM], axis=0, keepdims=True),
                    jnp.sum(inner[HDIM:], axis=0, keepdims=True),
                ],
                axis=1,
            )
            grad_rows = head_pair_rows(turned.T.astype(BF16))
            powered = powered_ref[member, :, columns]
            grad_powered = dot_nt(values_ref[tokens, lanes], grad_rows)
            grad_scores = (powered.astype(F32) * (grad_powered - inner_sum)).astype(BF16)
            made_values.append(dot_nn(powered, grad_rows))
            made_keys.append(dot_nn(grad_scores, head_pair_rows(queries_ref[tokens, lanes])))
            made_queries.append(head_pair_diagonal(dot_tn(keys_ref[tokens, lanes], grad_scores), SEQ).T)

    def assemble(pieces):
        return jnp.concatenate(
            [
                jnp.concatenate(pieces[member * PAIRS : (member + 1) * PAIRS], axis=1)
                for member in range(per_step)
            ],
            axis=0,
        ).astype(BF16)

    pull_queries[here, :] = assemble(made_queries)
    pull_keys[here, :] = assemble(made_keys)
    pull_values[here, :] = assemble(made_values)

    @pl.when(step == pl.num_programs(0) - 1)
    def _():
        rows = input_ref[...].astype(F32)
        scale = inverse_rms(rows)
        normed = (rows * scale * gain_ref[...]).astype(BF16)
        queries, keys, values = pull_queries[...], pull_keys[...], pull_values[...]
        store_turned(codes_ref[0], dot_tn(normed, queries), keep_a_ref, send_a_ref, 0, staged)
        store_turned(codes_ref[0], dot_tn(normed, keys), keep_a_ref, send_a_ref, 1, staged)
        store_turned(codes_ref[1], dot_tn(normed, values), keep_b_ref, send_b_ref, 0, staged)
        grad_normed = (
            dot_nt(queries, query_ref[...]) + dot_nt(keys, key_ref[...]) + dot_nt(values, value_ref[...])
        )
        grad_inputs_ref[...] = grad_all_ref[...] + norm_pull(rows, scale, gain_ref[...], grad_normed)


def self_backward(
    codes, grad_after, queries, keys, values, powered, inverse, blend, self_output, inputs, self_gain, self_query, self_key, self_value, after
):
    tokens, width = inputs.shape
    queries_here = tokens // SEQ
    per_step = 2 if queries_here % 2 == 0 else 1
    block = per_step * SEQ
    row_spec = pl.BlockSpec((block, width), lambda i, *_: (i, 0))
    weight = fixed((width, width))
    columns = HEADS * SEQ
    whole = fixed((tokens, width))

    def query_spec(*shape):
        return pl.BlockSpec((per_step,) + shape, lambda i, *_: (i, 0, 0))

    return functools.partial(call, cost=18)(
        functools.partial(self_pull_body, per_step),
        "self_backward",
        (queries_here // per_step,),
        [
            row_spec, row_spec, row_spec, row_spec,
            query_spec(SEQ, columns), query_spec(1, columns), query_spec(width, SEQ), weight,
            whole, whole, fixed((1, width)), weight, weight, weight,
        ],
        [whole] + [fixed((2, width // 2, width))] * 2 + [fixed((1, width // 2, width))] * 2,
        [shaped((tokens, width), F32)]
        + [shaped((2, width // 2, width), BF16)] * 2
        + [shaped((1, width // 2, width), BF16)] * 2,
        [pltpu.VMEM((tokens, width), BF16)] * 3 + [pltpu.VMEM((width, width), BF16)],
        prefetch=1,
        after=after,
    )(
        codes, grad_after, queries, keys, values, powered, inverse, blend, self_output,
        inputs, grad_after, self_gain, self_query, self_key, self_value,
    )


CHUNK = 256


def unit_of(unit):
    pair = unit % PAIRS
    return unit // PAIRS, slice(pair * PAIR, (pair + 1) * PAIR), slice(pair * 2 * SEQ, (pair + 1) * 2 * SEQ)


def fold_rows(values, operation):
    return operation(values.reshape(values.shape[0] // 8, 8, values.shape[1]), axis=0)


def cross_body(
    per_step, shared, chosen_ref, queries_ref, keys_ref, values_t_ref, ids_ref,
    powered_ref, inverse_ref, blend_ref, attended_ref, held,
):
    step = pl.program_id(0)
    slots = keys_ref.shape[1]
    chunks = [slice(start, start + CHUNK) for start in range(0, slots, CHUNK)]
    biases = []
    for member in range(per_step):
        ids = ids_ref[0 if shared else member]
        at = step * per_step + member
        seen = ids == chosen_ref[at, 0]
        for place in range(1, chosen_ref.shape[1]):
            seen = seen | (ids == chosen_ref[at, place])
        biases.append(jnp.where(seen, 0.0, MASKED).astype(F32))
    units = per_step * PAIRS
    queries, largest, totals, inverses = {}, {}, {}, {}
    for turn in range(units + 2):
        for at, rows in enumerate(chunks):
            unit = turn
            if unit < units:
                member, lanes, columns = unit_of(unit)
                pool = 0 if shared else member
                if at == 0:
                    queries[unit] = head_pair_rows(queries_ref[member * SEQ : (member + 1) * SEQ, lanes])
                bias = biases[member][rows]
                scores = dot_nt(keys_ref[pool, rows, lanes], queries[unit])
                scores = scores + jnp.concatenate([bias, bias], axis=1)
                held[unit % 2, rows, :] = scores
                high = fold_rows(scores, jnp.max)
                largest[unit] = high if at == 0 else jnp.maximum(largest[unit], high)
                if at == len(chunks) - 1:
                    largest[unit] = jnp.max(largest[unit], axis=0, keepdims=True)
            unit = turn - 1
            if 0 <= unit < units:
                member, lanes, columns = unit_of(unit)
                powered = jnp.exp(held[unit % 2, rows, :] - largest[unit])
                total = fold_rows(powered, jnp.sum)
                totals[unit] = total if at == 0 else totals[unit] + total
                powered_ref[member, rows, columns] = powered.astype(BF16)
                if at == len(chunks) - 1:
                    inverses[unit] = 1.0 / jnp.sum(totals[unit], axis=0, keepdims=True)
                    inverse_ref[member, :, columns] = inverses[unit]
            unit = turn - 2
            if 0 <= unit < units and at == len(chunks) - 1:
                member, lanes, columns = unit_of(unit)
                pool = 0 if shared else member
                blend = dot_nn(values_t_ref[pool, lanes, :], powered_ref[member, :, columns])
                blend = head_pair_diagonal(blend * inverses[unit], SEQ)
                blend_ref[member, lanes, :] = blend.astype(BF16)
                attended_ref[member * SEQ : (member + 1) * SEQ, lanes] = blend.T.astype(BF16)


def cross_forward(chosen, queries, keys, values_t, ids):
    tokens, width = queries.shape
    queries_here = tokens // SEQ
    shared = keys.shape[0] == 1
    slots = keys.shape[1]
    columns = HEADS * SEQ
    per_step = 2 if shared else 1

    def pool_spec(*shape):
        return fixed((1,) + shape) if shared else pl.BlockSpec((per_step,) + shape, lambda i, *_: (i, 0, 0))

    def query_spec(*shape):
        return pl.BlockSpec((per_step,) + shape, lambda i, *_: (i, 0, 0))

    row_spec = pl.BlockSpec((per_step * SEQ, width), lambda i, *_: (i, 0))
    return functools.partial(call, cost=20)(
        functools.partial(cross_body, per_step, shared),
        "cross_forward",
        (queries_here // per_step,),
        [row_spec, pool_spec(slots, width), pool_spec(width, slots), pool_spec(slots, SEQ)],
        [query_spec(slots, columns), query_spec(1, columns), query_spec(width, SEQ), row_spec],
        [
            shaped((queries_here, slots, columns), BF16),
            shaped((queries_here, 1, columns), F32),
            shaped((queries_here, width, SEQ), BF16),
            shaped((tokens, width), BF16),
        ],
        [pltpu.VMEM((2, slots, 2 * SEQ), F32)],
        prefetch=1,
    )(chosen, queries, keys, values_t, ids)


def feature_scale(inverse):
    return jnp.concatenate(
        [jnp.broadcast_to(inverse[:, :SEQ], (HDIM, SEQ)), jnp.broadcast_to(inverse[:, SEQ:], (HDIM, SEQ))], axis=0
    )


def feature_sums(values):
    return jnp.concatenate(
        [jnp.sum(values[:HDIM], axis=0, keepdims=True), jnp.sum(values[HDIM:], axis=0, keepdims=True)], axis=1
    )


def cross_pull_body(
    per_step, shared, grad_ref, queries_ref, keys_t_ref, values_ref, powered_ref, inverse_ref, blend_ref,
    pulled_ref, grad_keys_ref, grad_values_ref, held, keys_sum, values_sum,
):
    step = pl.program_id(0)
    last = pl.num_programs(0) - 1
    members = range(per_step)
    stack = per_step if shared else 1
    chunks = [slice(start, start + CHUNK) for start in range(0, values_ref.shape[1], CHUNK)]

    @pl.when(step == 0)
    def _():
        keys_sum[...] = jnp.zeros_like(keys_sum)
        values_sum[...] = jnp.zeros_like(values_sum)

    grads, sums, queries = [], [], []
    for member in members:
        tokens = slice(member * SEQ, (member + 1) * SEQ)
        turned = grad_ref[tokens, :].astype(F32).T * feature_scale(inverse_ref[member])
        sums.append(feature_sums(turned * blend_ref[member].astype(F32)))
        grads.append(head_pair_rows(turned.T.astype(BF16)))
        queries.append(head_pair_rows(queries_ref[tokens, :]))
    grads = jnp.concatenate(grads, axis=0)
    queries = jnp.concatenate(queries, axis=0)
    sums = jnp.concatenate(sums, axis=1)
    grad_powered = {}
    for at in range(len(chunks) + 1):
        if at < len(chunks):
            grad_powered[at] = dot_nt(values_ref[0, chunks[at], :], grads)
        if at:
            rows = chunks[at - 1]
            powered = jnp.concatenate([powered_ref[member, rows, :] for member in members], axis=1)
            held[rows, :] = (powered.astype(F32) * (grad_powered.pop(at - 1) - sums)).astype(BF16)
            values_sum[rows, :] += dot_nn(powered, grads)
            keys_sum[rows, :] += dot_nn(held[rows, :], queries)
    pulled = dot_nn(keys_t_ref[0], held[...])
    for member in members:
        mine = pulled[:, member * 2 * SEQ : (member + 1) * 2 * SEQ]
        pulled_ref[member * SEQ : (member + 1) * SEQ, :] = head_pair_diagonal(mine, SEQ).T.astype(BF16)
    if shared:

        @pl.when(step == last)
        def _():
            grad_keys_ref[0] = keys_sum[...].astype(grad_keys_ref.dtype)
            grad_values_ref[0] = values_sum[...].astype(grad_values_ref.dtype)

    else:
        grad_keys_ref[0] = keys_sum[...].astype(grad_keys_ref.dtype)
        grad_values_ref[0] = values_sum[...].astype(grad_values_ref.dtype)
        keys_sum[...] = jnp.zeros_like(keys_sum)
        values_sum[...] = jnp.zeros_like(values_sum)


def cross_backward(pair, grad_attended, queries, keys_t, values, powered, inverse, blend, after):
    tokens, width = queries.shape
    queries_here = tokens // SEQ
    pools, slots = values.shape[:2]
    shared = pools == 1
    per_step = 2 if shared else 1

    def pool_index(column):
        if shared:
            return lambda i: (0, pair, 0) if column else (0, 0, pair)
        return lambda i: (i, pair, 0) if column else (i, 0, pair)

    row_spec = pl.BlockSpec((per_step * SEQ, PAIR), lambda i: (i, pair))
    slot_spec = pl.BlockSpec((1, slots, PAIR), (lambda i: (0, 0, 0)) if shared else (lambda i: (i, 0, 0)))
    dtype = BF16 if shared else F32
    return call(
        functools.partial(cross_pull_body, per_step, shared),
        "cross_backward",
        (queries_here // per_step,),
        [
            row_spec, row_spec,
            pl.BlockSpec((1, PAIR, slots), pool_index(True)), pl.BlockSpec((1, slots, PAIR), pool_index(False)),
            pl.BlockSpec((per_step, slots, 2 * SEQ), lambda i: (i, 0, pair)),
            pl.BlockSpec((per_step, 1, 2 * SEQ), lambda i: (i, 0, pair)),
            pl.BlockSpec((per_step, PAIR, SEQ), lambda i: (i, pair, 0)),
        ],
        [pl.BlockSpec((per_step * SEQ, PAIR), lambda i: (i, 0)), slot_spec, slot_spec],
        [shaped((tokens, PAIR), BF16)] + [shaped((pools, slots, PAIR), dtype)] * 2,
        [
            pltpu.VMEM((slots, per_step * 2 * SEQ), BF16),
            pltpu.VMEM((slots, PAIR), F32), pltpu.VMEM((slots, PAIR), F32),
        ],
        cost=7,
        after=after,
    )(grad_attended, queries, keys_t, values, powered, inverse, blend)


def cross_close_body(
    codes_ref, pulled_0, pulled_1, pulled_2, pulled_3, after_ref, grad_cross_ref, gain_ref, query_ref, attended_ref,
    grad_after_ref, keep_ref, send_ref, staged,
):
    rows = after_ref[...]
    scale = inverse_rms(rows)
    normed = (rows * scale * gain_ref[...]).astype(BF16)
    pulled = jnp.concatenate([pulled_0[...], pulled_1[...], pulled_2[...], pulled_3[...]], axis=1)
    store_turned(codes_ref[0], dot_tn(normed, pulled), keep_ref, send_ref, 0, staged)
    grad_after = grad_cross_ref[...] + norm_pull(rows, scale, gain_ref[...], dot_nt(pulled, query_ref[...]))
    grad_after_ref[...] = grad_after
    grad_output = dot_tn(attended_ref[...], grad_after.astype(BF16))
    store_turned(codes_ref[0], grad_output, keep_ref, send_ref, 1, staged)


def cross_close(codes, pulled, after_self, grad_after_cross, cross_gain, cross_query, self_attended, after):
    tokens, width = after_self.shape
    weight = fixed((width, width))
    whole = fixed((tokens, width))
    half = fixed((2, width // 2, width))
    return call(
        cross_close_body,
        "cross_close",
        (1,),
        [fixed((tokens, PAIR))] * 4 + [whole, whole, fixed((1, width)), weight, whole],
        [whole, half, half],
        [shaped((tokens, width), F32)] + [shaped((2, width // 2, width), BF16)] * 2,
        [pltpu.VMEM((width, width), BF16)],
        prefetch=1,
        cost=6,
        after=after,
    )(codes, *pulled, after_self, grad_after_cross, cross_gain, cross_query, self_attended)


TANH_SLOPE = 0.7978845608028654
TANH_CUBE = 0.044715


def feed_body(
    limits_ref, codes_ref, after_ref, attended_ref, cotangent_ref, gain_ref, output_ref, inner_ref, outer_ref,
    layer_ref, grad_after_ref, grad_attended_ref, keep_a_ref, send_a_ref, keep_b_ref, send_b_ref, keep_c_ref, send_c_ref,
    after_cross, normed, grad_feed, total, grad_normed, staged,
):
    step = pl.program_id(0)
    tokens = after_cross.shape[0]

    @pl.when(step == 0)
    def _():
        rows = after_ref[...] + dot_nn(attended_ref[...], output_ref[...])
        after_cross[...] = rows
        total[...] = rows
        normed[...] = (rows * inverse_rms(rows) * gain_ref[...]).astype(BF16)
        grad_normed[...] = jnp.zeros_like(grad_normed)
        place = lax.broadcasted_iota(jnp.int32, (SEQ, cotangent_ref.shape[1]), 0)
        for member in range(tokens // SEQ):
            span = slice(member * SEQ, (member + 1) * SEQ)
            grads = cotangent_ref[span, :]
            grad_feed[span, :] = jnp.where(place < limits_ref[member], grads, jnp.zeros_like(grads))

    inner = inner_ref[...]
    outer = outer_ref[...]
    grads = grad_feed[...]
    pre = dot_nn(normed[...], inner)
    squared = pre * pre
    half = 0.5 * jnp.tanh(pre * (TANH_SLOPE + (TANH_SLOPE * TANH_CUBE) * squared)) + 0.5
    hidden = (pre * half).astype(BF16)
    slope = half + (pre * (2.0 * half * (1.0 - half))) * (
        TANH_SLOPE + (3.0 * TANH_SLOPE * TANH_CUBE) * squared
    )
    total[...] += dot_nn(hidden, outer)
    grad_pre = (dot_nt(grads, outer) * slope).astype(BF16)
    store_turned(codes_ref[0], dot_tn(hidden, grads), keep_a_ref, send_a_ref, 0, staged)
    store_turned(codes_ref[1], dot_tn(normed[...], grad_pre), keep_b_ref, send_b_ref, 0, staged)
    grad_normed[...] += dot_nt(grad_pre, inner)

    @pl.when(step == pl.num_programs(0) - 1)
    def _():
        layer_ref[...] = total[...].astype(BF16)
        rows = after_cross[...]
        scale = inverse_rms(rows)
        grad_rows = norm_pull(rows, scale, gain_ref[...], grad_normed[...])
        grad_after = grad_feed[...].astype(F32) + grad_rows
        grad_after_ref[...] = grad_after
        branch = grad_after.astype(BF16)
        store_turned(codes_ref[0], dot_tn(attended_ref[...], branch), keep_c_ref, send_c_ref, 0, staged)
        grad_attended_ref[...] = dot_nt(branch, output_ref[...]).astype(BF16)


def feed_both(limits, codes, after_self, attended, cotangent, feed_gain, cross_output, inner_weight, outer_weight):
    tokens, width = after_self.shape
    hidden = inner_weight.shape[1]
    block = width
    steps = hidden // block
    whole = fixed((tokens, width))
    weight = fixed((width, width))
    inner_spec = pl.BlockSpec((width, block), lambda i, *_: (0, i))
    outer_spec = pl.BlockSpec((block, width), lambda i, *_: (i, 0))
    half_spec = pl.BlockSpec((1, width // 2, width), lambda i, *_: (i, 0, 0))
    return functools.partial(call, cost=24)(
        feed_body,
        "feed_both",
        (steps,),
        [whole, whole, whole, fixed((1, width)), weight, inner_spec, outer_spec],
        [whole, whole, whole] + [half_spec] * 4 + [fixed((1, width // 2, width))] * 2,
        [shaped((tokens, width), BF16), shaped((tokens, width), F32), shaped((tokens, width), BF16)]
        + [shaped((steps, width // 2, width), BF16)] * 4
        + [shaped((1, width // 2, width), BF16)] * 2,
        [
            pltpu.VMEM((tokens, width), F32), pltpu.VMEM((tokens, width), BF16), pltpu.VMEM((tokens, width), BF16),
            pltpu.VMEM((tokens, width), F32), pltpu.VMEM((tokens, width), F32),
            pltpu.VMEM((width, width), BF16),
        ],
        prefetch=2,
    )(limits, codes, after_self, attended, cotangent, feed_gain, cross_output, inner_weight, outer_weight)


def permute(values, batch_bits, mem_bits):
    if batch_bits:
        axis, bits, count = "batch", batch_bits, lax.axis_size("batch")
    else:
        axis, bits, count = "mem", mem_bits, lax.axis_size("mem")
    return lax.ppermute(values, axis, [(at, at ^ bits) for at in range(count)])


CORE, ACROSS, ALONG = (1, 0), (2, 0), (0, 1)
DEEP = ((0, 2), (0, 4), (0, 6))


def added(*terms):
    total = terms[0].astype(F32)
    for term in terms[1:]:
        total = total + term.astype(F32)
    return total.astype(BF16)


def portions(count, *terms):
    size = terms[0].shape[1] // count
    return [added(*[t[:, i * size : (i + 1) * size] for t in terms]) for i in range(count)]


def beyond(values):
    bits = 8
    while bits < lax.axis_size("mem"):
        values = added(values, permute(values, 0, bits))
        bits *= 2
    return values


def reduce_all(keep_a, send_a, keep_b, send_b):
    count = keep_a.shape[0]
    got_a, got_b = permute(send_a, *CORE), permute(send_b, *CORE)
    keep_a, send_a = portions(2, keep_a, got_a)
    keep_b, send_b = portions(2, keep_b, got_b)
    yield (send_a, send_b)
    got_a, got_b = permute(send_a, *ACROSS), permute(send_b, *ALONG)
    keep_a, send_a = portions(2, keep_a, got_a)
    keep_b, send_b = portions(2, keep_b, got_b)
    yield (send_a, send_b)
    got_a, got_b = permute(send_a, *ALONG), permute(send_b, *ACROSS)
    parts_a = portions(4, keep_a, got_a)
    parts_b = portions(4, keep_b, got_b)
    parts = [jnp.concatenate([a, b], axis=0) for a, b in zip(parts_a, parts_b)]
    yield tuple(parts[1:])
    own = beyond(added(parts[0], *[permute(p, *bits) for p, bits in zip(parts[1:], DEEP)]))
    yield (own,)
    whole = jnp.concatenate([own] + [permute(own, *bits) for bits in DEEP], axis=1)
    whole_a, whole_b = whole[:count], whole[count:]
    yield (whole_a, whole_b)
    got_a, got_b = permute(whole_a, *ALONG), permute(whole_b, *ACROSS)
    whole_a = jnp.concatenate([whole_a, got_a], axis=1)
    whole_b = jnp.concatenate([whole_b, got_b], axis=1)
    yield (whole_a, whole_b)
    got_a, got_b = permute(whole_a, *ACROSS), permute(whole_b, *ALONG)
    whole_a = jnp.concatenate([whole_a, got_a], axis=1)
    whole_b = jnp.concatenate([whole_b, got_b], axis=1)
    yield (whole_a, whole_b)
    return whole_a, permute(whole_a, *CORE), whole_b, permute(whole_b, *CORE)


class Sum:
    def __init__(self, *arrays):
        self.steps = reduce_all(*arrays)
        self.result = None

    def step(self):
        try:
            return next(self.steps)
        except StopIteration as stop:
            self.result = stop.value
            return tuple(stop.value)


def advance(*sums):
    arrays = ()
    for member in sums:
        if member.result is None:
            arrays = arrays + tuple(member.step())
    return arrays


def restore(code, own, other, at, target, rows):
    size = 2 * own.shape[1] // BLOCKS
    half = BLOCKS // 2
    for place in range(BLOCKS):
        source = own if place < half else other
        start = (place % half) * size
        goal = pl.ds(pl.multiple_of((place ^ code) * size + rows, size), size)
        target[goal, :] = source[at, start : start + size, :].astype(F32)


def fold_lanes(values):
    total = values[:, :128]
    for start in range(128, values.shape[1], 128):
        total = total + values[:, start : start + 128]
    return total


def restore_stack_body(codes_ref, own_ref, other_ref, out_ref):
    restore(codes_ref[0], own_ref, other_ref, 0, out_ref, 0)


def restore_rows(codes, own, other):
    count, half, width = own.shape
    spec = pl.BlockSpec((1, half, width), lambda i, *_: (i, 0, 0))
    return functools.partial(call, cost=5)(
        restore_stack_body, "restore_rows", (count,), [spec, spec],
        pl.BlockSpec((2 * half, width), lambda i, *_: (i, 0)),
        shaped((count * 2 * half, width), F32), prefetch=1,
    )(codes, own, other)


def restore_columns_body(codes_ref, own_ref, other_ref, weight_ref, gain_ref, out_ref, grad_gain_ref, sums):
    step = pl.program_id(0)

    @pl.when(step == 0)
    def _():
        sums[...] = jnp.zeros_like(sums)

    restore(codes_ref[1], own_ref, other_ref, 0, out_ref, 0)
    sums[...] += fold_lanes(out_ref[...] * weight_ref[...].astype(F32))

    @pl.when(step == pl.num_programs(0) - 1)
    def _():
        grad_gain_ref[...] = jnp.sum(sums[...].T, axis=0, keepdims=True) / gain_ref[...]


def restore_columns(codes, own, other, weight, gain):
    count, half, width = own.shape
    spec = pl.BlockSpec((1, half, width), lambda i, *_: (i, 0, 0))
    wide = pl.BlockSpec((2 * half, width), lambda i, *_: (0, i))
    return functools.partial(call, cost=6)(
        restore_columns_body, "restore_columns", (count,), [spec, spec, wide, fixed((1, 2 * half))],
        [wide, fixed((1, 2 * half))],
        [shaped((2 * half, count * width), F32), shaped((1, 2 * half), F32)],
        [pltpu.VMEM((2 * half, 128), F32)], prefetch=1,
    )(codes, own, other, weight, gain)


def restore_cross_body(
    codes_ref, own_a_ref, other_a_ref, own_b_ref, other_b_ref, query_ref, key_ref, value_ref, cross_gain_ref, encoder_gain_ref,
    output_out, query_out, self_out, key_out, value_out, cross_gain_out, encoder_gain_out,
):
    restore(codes_ref[0], own_a_ref, other_a_ref, 0, output_out, 0)
    restore(codes_ref[0], own_a_ref, other_a_ref, 1, query_out, 0)
    restore(codes_ref[0], own_a_ref, other_a_ref, 2, self_out, 0)
    restore(codes_ref[1], own_b_ref, other_b_ref, 0, key_out, 0)
    restore(codes_ref[1], own_b_ref, other_b_ref, 1, value_out, 0)
    sums = fold_lanes(query_out[...] * query_ref[...].astype(F32))
    cross_gain_out[...] = jnp.sum(sums.T, axis=0, keepdims=True) / cross_gain_ref[...]
    sums = fold_lanes(
        key_out[...] * key_ref[...].astype(F32) + value_out[...] * value_ref[...].astype(F32)
    )
    encoder_gain_out[...] = jnp.sum(sums.T, axis=0, keepdims=True) / encoder_gain_ref[...]


def restore_cross(codes, own_a, other_a, own_b, other_b, cross_query, cross_key, cross_value, cross_gain, encoder_gain):
    width = own_a.shape[2]
    weight, row = fixed((width, width)), fixed((1, width))
    return functools.partial(call, cost=5)(
        restore_cross_body, "restore_cross", (1,),
        [fixed(own_a.shape)] * 2 + [fixed(own_b.shape)] * 2 + [weight] * 3 + [row] * 2,
        [weight] * 5 + [row] * 2,
        [shaped((width, width), F32)] * 5 + [shaped((1, width), F32)] * 2, prefetch=1,
    )(codes, own_a, other_a, own_b, other_b, cross_query, cross_key, cross_value, cross_gain, encoder_gain)


def restore_self_body(
    codes_ref, own_a_ref, other_a_ref, own_b_ref, other_b_ref, query_ref, key_ref, value_ref, gain_ref,
    query_out, key_out, value_out, gain_out,
):
    restore(codes_ref[0], own_a_ref, other_a_ref, 0, query_out, 0)
    restore(codes_ref[0], own_a_ref, other_a_ref, 1, key_out, 0)
    restore(codes_ref[1], own_b_ref, other_b_ref, 0, value_out, 0)
    sums = fold_lanes(
        query_out[...] * query_ref[...].astype(F32)
        + key_out[...] * key_ref[...].astype(F32)
        + value_out[...] * value_ref[...].astype(F32)
    )
    gain_out[...] = jnp.sum(sums.T, axis=0, keepdims=True) / gain_ref[...]


def restore_self(codes, own_a, other_a, own_b, other_b, self_query, self_key, self_value, self_gain):
    width = own_a.shape[2]
    weight, row = fixed((width, width)), fixed((1, width))
    return functools.partial(call, cost=4)(
        restore_self_body, "restore_self", (1,),
        [fixed(own_a.shape)] * 2 + [fixed(own_b.shape)] * 2 + [weight] * 3 + [row],
        [weight] * 3 + [row],
        [shaped((width, width), F32)] * 3 + [shaped((1, width), F32)], prefetch=1,
    )(codes, own_a, other_a, own_b, other_b, self_query, self_key, self_value, self_gain)


def device_codes():
    batch_at, mem_at = lax.axis_index("batch"), lax.axis_index("mem")
    core, across = batch_at & 1, batch_at >> 1
    along, deep = mem_at & 1, (mem_at >> 1) & 3
    return jnp.stack(
        [
            (core << 4) | (across << 3) | (along << 2) | deep,
            (core << 4) | (along << 3) | (across << 2) | deep,
        ]
    ).astype(jnp.int32)


def passage_slots(pool_ids, chosen, passages, pool_rows):
    passage_marks = jnp.arange(passages, dtype=jnp.int32)
    starts = jnp.sum(
        (pool_ids[None, :] < passage_marks[:, None]).astype(jnp.int32), axis=1, dtype=jnp.int32
    )
    counts = jnp.sum(
        (pool_ids[None, :] == passage_marks[:, None]).astype(jnp.int32), axis=1, dtype=jnp.int32
    )
    picked = (chosen[..., None] == passage_marks).astype(jnp.int32)
    first_row = jnp.sum(picked * starts, axis=-1, dtype=jnp.int32)
    extent = jnp.sum(picked * counts, axis=-1, dtype=jnp.int32)
    offsets = jnp.arange(PLEN, dtype=jnp.int32)
    slot_rows = jnp.minimum(first_row[..., None] + offsets, pool_rows - 1)
    slot_visible = offsets < extent[..., None]
    slot_shape = (chosen.shape[0], chosen.shape[1] * PLEN)
    return (slot_rows.reshape(slot_shape), slot_visible.reshape(slot_shape))


def local(
    inputs,
    cotangent,
    memory,
    passage_ids,
    retrieved,
    task_ids,
    target_lens,
    encoder_gain,
    self_gain,
    cross_gain,
    feed_gain,
    self_query,
    self_key,
    self_value,
    self_output,
    cross_query,
    cross_key,
    cross_value,
    cross_output,
    inner_weight,
    outer_weight,
):
    width = inputs.shape[2]
    own_rows = memory.shape[1]
    chosen = retrieved[0]
    codes = device_codes()
    encoder_row, self_row, cross_row, feed_row = (
        member.reshape(1, width) for member in (encoder_gain, self_gain, cross_gain, feed_gain)
    )
    pool_memory = lax.all_gather(memory[0], "mem", axis=0, tiled=True)
    pool_ids = lax.all_gather(passage_ids[0], "mem", axis=0, tiled=True)
    pool_rows = pool_memory.shape[0]
    (
        self_queries, self_keys, self_values, self_powered, self_inverse, self_blend,
        self_attended, after_self, cross_queries,
    ) = self_forward(
        inputs[0], self_row, cross_row, self_query, self_key, self_value, self_output, cross_query
    )
    pool_keys, pool_values, pool_keys_t, pool_values_t = memory_forward(
        pool_memory, encoder_row, cross_key, cross_value
    )
    slots = chosen.shape[1] * PLEN
    shared = pool_rows <= slots
    if shared:
        keys, values = pool_keys[None], pool_values[None]
        keys_t, values_t = pool_keys_t[None], pool_values_t[None]
        ids = pool_ids[None]
    else:
        passages = PASS_DEV * lax.axis_size("mem")
        slot_rows, slot_visible = passage_slots(pool_ids, chosen, passages, pool_rows)
        keys = jnp.take(pool_keys, slot_rows, axis=0)
        values = jnp.take(pool_values, slot_rows, axis=0)
        keys_t, values_t = jnp.swapaxes(keys, 1, 2), jnp.swapaxes(values, 1, 2)
        ids = jnp.where(slot_visible, jnp.take(pool_ids, slot_rows), -1)
    ids = jnp.broadcast_to(ids[..., None], ids.shape + (SEQ,))
    cross_powered, cross_inverse, cross_blend, cross_attended = cross_forward(
        chosen, cross_queries, keys, values_t, ids
    )
    limits = jnp.minimum(target_lens[0], SEQ - task_ids[0] * (SEQ // 4))
    (
        layer_out, grad_after_cross, grad_cross_attended, outer_keep, outer_send, inner_keep, inner_send,
        output_keep, output_send,
    ) = feed_both(
        limits, codes, after_self, cross_attended, cotangent[0], feed_row, cross_output, inner_weight, outer_weight
    )
    feed_sum = Sum(outer_keep, outer_send, inner_keep, inner_send)
    held = ()
    pieces = []
    for pair in range(PAIRS):
        now = advance(feed_sum)
        pieces.append(
            cross_backward(
                pair, grad_cross_attended, cross_queries, keys_t, values, cross_powered, cross_inverse, cross_blend, held
            )
        )
        held = now
    now = advance(feed_sum)
    grad_after_self, query_keep, query_send = cross_close(
        codes, [piece[0] for piece in pieces], after_self, grad_after_cross, cross_row, cross_query, self_attended, held
    )
    held = now
    grad_keys, grad_values = [piece[1] for piece in pieces], [piece[2] for piece in pieces]
    if shared:
        pool_grads = [[member[0] for member in members] for members in (grad_keys, grad_values)]
    else:
        slot_index = jnp.where(slot_visible, slot_rows, pool_rows).reshape(-1)
        empty = jnp.zeros((pool_rows, PAIR), F32)
        pool_grads = [
            [empty.at[slot_index].add(member.reshape(-1, PAIR), mode="drop") for member in members]
            for members in (grad_keys, grad_values)
        ]
    grad_pool_normed, pool_keep, pool_send = memory_backward(
        codes, pool_memory, encoder_row, cross_key, cross_value, *pool_grads, ()
    )
    cross_sum = Sum(
        jnp.concatenate([output_keep, query_keep], axis=0),
        jnp.concatenate([output_send, query_send], axis=0),
        pool_keep,
        pool_send,
    )
    grad_own_normed = lax.psum_scatter(grad_pool_normed, "mem", scatter_dimension=0, tiled=True)
    memory_rows = memory[0].astype(F32)
    grad_memory = norm_pull(
        memory_rows, inverse_rms(memory_rows), encoder_row, grad_own_normed.astype(F32)
    )
    now = advance(feed_sum, cross_sum)
    grad_inputs, self_keep_a, self_send_a, self_keep_b, self_send_b = self_backward(
        codes, grad_after_self, self_queries, self_keys, self_values, self_powered, self_inverse, self_blend,
        self_output, inputs[0], self_row, self_query, self_key, self_value, held,
    )
    self_sum = Sum(self_keep_a, self_send_a, self_keep_b, self_send_b)
    while feed_sum.result is None:
        advance(feed_sum, cross_sum, self_sum)
    grad_outer = restore_rows(codes, feed_sum.result[0], feed_sum.result[1])
    grad_inner, grad_feed_gain = restore_columns(
        codes, feed_sum.result[2], feed_sum.result[3], inner_weight, feed_row
    )
    while cross_sum.result is None:
        advance(cross_sum, self_sum)
    (
        grad_cross_output, grad_cross_query, grad_self_output, grad_cross_key, grad_cross_value,
        grad_cross_gain, grad_encoder_gain,
    ) = restore_cross(
        codes, *cross_sum.result, cross_query, cross_key, cross_value, cross_row, encoder_row
    )
    while self_sum.result is None:
        advance(self_sum)
    grad_self_query, grad_self_key, grad_self_value, grad_self_gain = restore_self(
        codes, *self_sum.result, self_query, self_key, self_value, self_row
    )
    return (
        layer_out[None],
        grad_inputs[None],
        grad_memory[None],
        grad_encoder_gain[0],
        grad_self_gain[0],
        grad_cross_gain[0],
        grad_feed_gain[0],
        grad_self_query,
        grad_self_key,
        grad_self_value,
        grad_self_output,
        grad_cross_query,
        grad_cross_key,
        grad_cross_value,
        grad_cross_output,
        grad_inner,
        grad_outer,
    )


def solution(mesh):
    spread = (P("batch", "mem", None),) * 3
    in_specs = spread + (
        P("batch", "mem"), P("batch", "mem", None), P("batch", "mem"), P("batch", "mem"),
    ) + (P(),) * 14
    out_specs = spread + (P(),) * 14
    return jax.shard_map(local, mesh=mesh, in_specs=in_specs, out_specs=out_specs, check_vma=False)
```

```python
import functools

import jax
import jax.numpy as jnp
from jax import lax
from jax.experimental import pallas as pl
from jax.experimental.pallas import tpu as pltpu
from jax.sharding import PartitionSpec as P

HEADS = 8
HDIM = 64
SEQ = 128
PLEN = 256
PASS_DEV = 1
PAIRS = HEADS // 2
PAIR = 2 * HDIM

EPSILON = 1e-06
MASKED = -1e30
F32 = jnp.float32
BF16 = jnp.bfloat16
MIB = 1024 * 1024
BLOCKS = 32


def dot_nn(former, latter):
    return lax.dot_general(
        former, latter, (((1,), (0,)), ((), ())), preferred_element_type=F32
    )


def dot_tn(former, latter):
    return lax.dot_general(
        former, latter, (((0,), (0,)), ((), ())), preferred_element_type=F32
    )


def dot_nt(former, latter):
    return lax.dot_general(
        former, latter, (((1,), (1,)), ((), ())), preferred_element_type=F32
    )


def inverse_rms(values):
    return lax.rsqrt(jnp.mean(values * values, axis=-1, keepdims=True) + EPSILON)


def norm_pull(values, row_scale, norm_gain, grad_normed):
    weighted = grad_normed * norm_gain
    cubed = row_scale * row_scale * row_scale
    grad_values = row_scale * weighted - values * (
        cubed * jnp.mean(values * weighted, axis=-1, keepdims=True)
    )
    return grad_values


def head_pair_rows(values):
    lane = lax.broadcasted_iota(jnp.int32, values.shape, 1)
    zero = jnp.zeros_like(values)
    return jnp.concatenate(
        [jnp.where(lane < HDIM, values, zero), jnp.where(lane < HDIM, zero, values)], axis=0
    )


def head_pair_diagonal(values, rows):
    return jnp.concatenate([values[:HDIM, :rows], values[HDIM:, rows:]], axis=0)


def store_turned(code, value, keep_ref, send_ref, at, staged):
    staged[...] = value.astype(BF16)
    blocks = BLOCKS
    size = value.shape[0] // blocks
    for place in range(blocks):
        source = pl.ds(pl.multiple_of((place ^ code) * size, size), size)
        half = blocks // 2
        target = keep_ref if place < half else send_ref
        start = (place % half) * size
        target[at, start : start + size, :] = staged[source, :]


def store_wide(code, staged, keep_ref, send_ref):
    size = staged.shape[0] // BLOCKS
    for place in range(BLOCKS):
        source = pl.ds(pl.multiple_of((place ^ code) * size, size), size)
        half = BLOCKS // 2
        target = keep_ref if place < half else send_ref
        start = (place % half) * size
        target[0, start : start + size, :] = staged[source, :]


def call(body, name, grid, in_specs, out_specs, out_shape, scratch=(), prefetch=0, vmem=56, cost=5, after=()):
    first = prefetch + len(in_specs)

    def waiting(*refs):
        body(*refs[:first], *refs[first + len(after) :])

    kernel = pl.pallas_call(
        waiting,
        name=name,
        grid_spec=pltpu.PrefetchScalarGridSpec(
            num_scalar_prefetch=prefetch,
            grid=grid,
            in_specs=list(in_specs) + [pl.BlockSpec(memory_space=pl.ANY)] * len(after),
            out_specs=out_specs,
            scratch_shapes=list(scratch),
        ),
        out_shape=out_shape,
        cost_estimate=pl.CostEstimate(flops=int(cost * 1.15e8), bytes_accessed=0, transcendentals=0),
        compiler_params=pltpu.CompilerParams(
            vmem_limit_bytes=vmem * MIB,
            dimension_semantics=("arbitrary",) * len(grid),
        ),
    )
    return lambda *operands: kernel(*operands, *after)


def resident(body, name, operands, outs, scratch=(), scalars=0, vmem=16, cost=5):
    whole, scalar = pl.BlockSpec(memory_space=pltpu.VMEM), pl.BlockSpec(memory_space=pltpu.SMEM)
    return pl.pallas_call(
        body,
        name=name,
        in_specs=[scalar] * scalars + [whole] * (len(operands) - scalars),
        out_specs=[whole] * len(outs),
        out_shape=list(outs),
        scratch_shapes=list(scratch),
        cost_estimate=pl.CostEstimate(flops=int(cost * 1.15e8), bytes_accessed=0, transcendentals=0),
        compiler_params=pltpu.CompilerParams(vmem_limit_bytes=vmem * MIB),
    )(*operands)


def fixed(shape):
    return pl.BlockSpec(shape, lambda *_: (0,) * len(shape), pipeline_mode=pl.Buffered(1))


def shaped(shape, dtype):
    return jax.ShapeDtypeStruct(shape, dtype)


def near(shape, dtype):
    return pltpu.VMEM(shape, dtype)


def streamed(values):
    return pltpu.with_memory_space_constraint(values, pltpu.HBM)


def far(shape, dtype):
    return pltpu.HBM(shape, dtype)


def memory_body(memory_ref, gain_ref, key_ref, value_ref, keys_ref, values_ref, keys_t_ref, values_t_ref):
    rows = memory_ref[...].astype(F32)
    normed = (rows * inverse_rms(rows) * gain_ref[...]).astype(BF16)
    keys_ref[...] = dot_nn(normed, key_ref[...]).astype(BF16)
    values_ref[...] = dot_nn(normed, value_ref[...]).astype(BF16)
    keys_t_ref[...] = lax.dot_general(
        key_ref[...], normed, (((0,), (1,)), ((), ())), preferred_element_type=F32
    ).astype(BF16)
    values_t_ref[...] = lax.dot_general(
        value_ref[...], normed, (((0,), (1,)), ((), ())), preferred_element_type=F32
    ).astype(BF16)


def memory_forward(memory, encoder_gain, cross_key, cross_value):
    count, width = memory.shape
    block = 512 if count % 512 == 0 else count
    kind = near if count <= 1024 else far
    row_spec = pl.BlockSpec((block, width), lambda i: (i, 0))
    column_spec = pl.BlockSpec((width, block), lambda i: (0, i))
    return functools.partial(call, cost=5, vmem=16)(
        memory_body,
        "memory_forward",
        (count // block,),
        [row_spec, fixed((1, width)), fixed(cross_key.shape), fixed(cross_value.shape)],
        [row_spec, row_spec, column_spec, column_spec],
        [kind((count, width), BF16)] * 2 + [kind((width, count), BF16)] * 2,
    )(memory, encoder_gain, cross_key, cross_value)


def memory_blocks_body(own_rows, gain_ref, key_ref, value_ref, *refs):
    count = len(refs) - 6
    blocks = refs[:count]
    pool_ref, ids_ref, keys_ref, values_ref, keys_t_ref, values_t_ref = refs[count:]
    for at, block in enumerate(blocks):
        here = slice(at * own_rows, (at + 1) * own_rows)
        pool_ref[here, :] = block[:own_rows, :]
        marks = block[own_rows : own_rows + 1, :own_rows].astype(F32)
        ids_ref[0, here, :] = jnp.broadcast_to(marks, (own_rows, own_rows)).T.astype(jnp.int32)
    memory_body(pool_ref, gain_ref, key_ref, value_ref, keys_ref, values_ref, keys_t_ref, values_t_ref)


def memory_blocks(blocks, own_rows, encoder_gain, cross_key, cross_value):
    count, width = own_rows * len(blocks), blocks[0].shape[1]
    return resident(
        functools.partial(memory_blocks_body, own_rows),
        "memory_blocks",
        (encoder_gain, cross_key, cross_value, *blocks),
        [near((count, width), BF16), near((1, count, own_rows), jnp.int32)]
        + [near((count, width), BF16)] * 2 + [near((width, count), BF16)] * 2,
        cost=3,
    )


def memory_pull_body(
    own_rows, once, codes_ref, memory_ref, gain_ref, key_ref, value_ref, keys_0, keys_1, keys_2, keys_3, values_0, values_1, values_2, values_3,
    grad_normed_ref, keep_ref, send_ref, grad_key, grad_value, staged,
):
    rows = memory_ref[...].astype(F32)
    normed = (rows * inverse_rms(rows) * gain_ref[...]).astype(BF16)
    grad_keys = jnp.concatenate([keys_0[...], keys_1[...], keys_2[...], keys_3[...]], axis=1).astype(BF16)
    grad_values = jnp.concatenate([values_0[...], values_1[...], values_2[...], values_3[...]], axis=1).astype(BF16)
    grad_normed = dot_nt(grad_keys, key_ref[...]) + dot_nt(grad_values, value_ref[...])
    held = rows.shape[0] // own_rows
    step = 0 if once else pl.program_id(0)
    for place in range(held):
        goal = ((step * held + place) ^ codes_ref[2]) * own_rows
        goal = pl.ds(pl.multiple_of(goal, own_rows), own_rows)
        grad_normed_ref[goal, :] = grad_normed[place * own_rows : (place + 1) * own_rows].astype(BF16)

    def store():
        store_turned(codes_ref[0], grad_key[...], keep_ref, send_ref, 0, staged)
        store_turned(codes_ref[0], grad_value[...], keep_ref, send_ref, 1, staged)

    if once:
        grad_key[...] = dot_tn(normed, grad_keys)
        grad_value[...] = dot_tn(normed, grad_values)
        store()
        return

    @pl.when(step == 0)
    def _():
        grad_key[...] = jnp.zeros_like(grad_key)
        grad_value[...] = jnp.zeros_like(grad_value)

    grad_key[...] += dot_tn(normed, grad_keys)
    grad_value[...] += dot_tn(normed, grad_values)
    pl.when(step == pl.num_programs(0) - 1)(store)


def memory_backward(own_rows, codes, memory, encoder_gain, cross_key, cross_value, grad_keys, grad_values):
    count, width = memory.shape
    if count <= 1024:
        return resident(
            functools.partial(memory_pull_body, own_rows, True),
            "memory_backward",
            (codes, memory, encoder_gain, cross_key, cross_value, *grad_keys, *grad_values),
            [near((count, width), BF16)] + [near((2, width // 2, width), BF16)] * 2,
            [pltpu.VMEM((width, width), F32)] * 2 + [pltpu.VMEM((width, width), BF16)],
            scalars=1, cost=3,
        )
    block = 1024 if count % 1024 == 0 else count
    row_spec = pl.BlockSpec((block, width), lambda i, *_: (i, 0))
    half = fixed((2, width // 2, width))
    return functools.partial(call, cost=7, vmem=48)(
        functools.partial(memory_pull_body, own_rows, False),
        "memory_backward",
        (count // block,),
        [row_spec, fixed((1, width)), fixed(cross_key.shape), fixed(cross_value.shape)] + [pl.BlockSpec((block, PAIR), lambda i, *_: (i, 0))] * 8,
        [fixed((count, width)), half, half],
        [shaped((count, width), BF16)] + [shaped((2, width // 2, width), BF16)] * 2,
        [pltpu.VMEM((width, width), F32)] * 2 + [pltpu.VMEM((width, width), BF16)],
        prefetch=1,
    )(codes, *map(streamed, (memory,)), encoder_gain, *map(streamed, (cross_key, cross_value, *grad_keys, *grad_values)))


def causal_bias():
    key_at = lax.broadcasted_iota(jnp.int32, (SEQ, 2 * SEQ), 0)
    query_at = lax.broadcasted_iota(jnp.int32, (SEQ, 2 * SEQ), 1) % SEQ
    return jnp.where(key_at <= query_at, 0.0, MASKED).astype(F32)


def softmax_columns(scores):
    largest = jnp.max(scores, axis=0, keepdims=True)
    powered = jnp.exp(scores - largest)
    inverse = 1.0 / jnp.sum(powered, axis=0, keepdims=True)
    return powered.astype(BF16), inverse


def self_open_body(input_hbm, query_hbm, key_hbm, value_hbm, gain_ref, queries_ref, keys_ref, values_ref, input_ref, *refs):
    weights, signals = refs[:3], refs[3]
    copies = []
    for source, target in zip((input_hbm, query_hbm, key_hbm, value_hbm), (input_ref, *weights)):
        copies.append(pltpu.make_async_copy(source, target, signals.at[len(copies)]))
        copies[-1].start()
    copies[0].wait()
    rows = input_ref[...].astype(F32)
    normed = (rows * inverse_rms(rows) * gain_ref[...]).astype(BF16)
    for copy, weight, target in zip(copies[1:], weights, (queries_ref, keys_ref, values_ref)):
        copy.wait()
        target[...] = dot_nn(normed, weight[...]).astype(BF16)


def self_open(inputs, self_gain, self_query, self_key, self_value):
    tokens, width = inputs.shape
    whole, anywhere = pl.BlockSpec(memory_space=pltpu.VMEM), pl.BlockSpec(memory_space=pl.ANY)
    return pl.pallas_call(
        self_open_body,
        name="self_open",
        in_specs=[anywhere] * 4 + [whole],
        out_specs=[whole] * 3,
        out_shape=[near((tokens, width), BF16)] * 3,
        scratch_shapes=[pltpu.VMEM((tokens, width), BF16)]
        + [pltpu.VMEM((width, width), BF16)] * 3
        + [pltpu.SemaphoreType.DMA((4,))],
        cost_estimate=pl.CostEstimate(flops=int(3 * 1.15e8), bytes_accessed=0, transcendentals=0),
        compiler_params=pltpu.CompilerParams(vmem_limit_bytes=16 * MIB),
    )(*map(streamed, (inputs, self_query, self_key, self_value)), self_gain)


def self_body(
    input_ref, cross_gain_ref, queries_ref, keys_ref, values_ref, output_ref, cross_ref,
    queries_out, keys_out, values_out, powered_out, inverse_ref, blend_out, attended_out, after_ref, cross_queries_ref,
    powered_ref, blend_ref, attended_ref, signals,
):
    moves = []

    def move(source, target):
        moves.append(pltpu.make_async_copy(source, target, signals.at[len(moves)]))
        moves[-1].start()

    move(queries_ref, queries_out)
    move(keys_ref, keys_out)
    move(values_ref, values_out)
    bias = causal_bias()
    members = input_ref.shape[0] // SEQ
    scores = {}
    for turn in range(members + 1):
        if turn < members:
            tokens = slice(turn * SEQ, (turn + 1) * SEQ)
            for pair in range(PAIRS):
                _, lanes, columns = unit_of(pair)
                scores[turn, pair] = bias + dot_nt(keys_ref[tokens, lanes], head_pair_rows(queries_ref[tokens, lanes]))
        if turn:
            member = turn - 1
            tokens = slice(member * SEQ, (member + 1) * SEQ)
            made = []
            for pair in range(PAIRS):
                _, lanes, columns = unit_of(pair)
                powered, inverse = softmax_columns(scores.pop((member, pair)))
                powered_ref[member, :, columns] = powered
                inverse_ref[member, :, columns] = inverse
                made.append((powered, inverse))
            for pair in range(PAIRS):
                _, lanes, columns = unit_of(pair)
                powered, inverse = made[pair]
                blend = head_pair_diagonal(dot_tn(values_ref[tokens, lanes], powered) * inverse, SEQ)
                blend_ref[member, lanes, :] = blend.astype(BF16)
                attended_ref[tokens, lanes] = blend.T.astype(BF16)
    move(powered_ref, powered_out)
    move(blend_ref, blend_out)
    move(attended_ref, attended_out)
    for start in range(0, input_ref.shape[0], 256):
        span = slice(start, start + 256)
        after = input_ref[span, :].astype(F32) + dot_nn(attended_ref[span, :], output_ref[...])
        after_ref[span, :] = after
        cross_normed = (after * inverse_rms(after) * cross_gain_ref[...]).astype(BF16)
        cross_queries_ref[span, :] = dot_nn(cross_normed, cross_ref[...]).astype(BF16)
    for copy in moves:
        copy.wait()


def self_forward(inputs, cross_gain, queries, keys, values, self_output, cross_query):
    tokens, width = inputs.shape
    queries_here = tokens // SEQ
    columns = HEADS * SEQ
    whole, anywhere = pl.BlockSpec(memory_space=pltpu.VMEM), pl.BlockSpec(memory_space=pl.ANY)
    shapes = [(queries_here, SEQ, columns), (queries_here, width, SEQ), (tokens, width)]
    return pl.pallas_call(
        self_body,
        name="self_forward",
        in_specs=[whole] * 7,
        out_specs=[anywhere] * 4 + [whole] + [anywhere] * 2 + [whole] * 2,
        out_shape=[far((tokens, width), BF16)] * 3
        + [far(shapes[0], BF16), near((queries_here, 1, columns), F32)]
        + [far(shape, BF16) for shape in shapes[1:]]
        + [near((tokens, width), F32), near((tokens, width), BF16)],
        scratch_shapes=[pltpu.VMEM(shape, BF16) for shape in shapes] + [pltpu.SemaphoreType.DMA((6,))],
        cost_estimate=pl.CostEstimate(flops=int(6 * 1.15e8), bytes_accessed=0, transcendentals=0),
        compiler_params=pltpu.CompilerParams(vmem_limit_bytes=20 * MIB),
    )(inputs, cross_gain, queries, keys, values, self_output, cross_query)


def self_pull_body(
    last_piece, codes_ref, grad_ref, queries_ref, keys_ref, values_ref, powered_ref, inverse_ref, blend_ref, output_ref,
    *refs,
):
    if last_piece:
        former_ref, input_ref, gain_ref, pulled_ref, keep_ref, send_ref, staged, grad_attended = refs
        start = former_ref.shape[0]
        pulled_ref[:start, :] = former_ref[...]
    else:
        pulled_ref, grad_attended = refs
        start = 0
    width = queries_ref.shape[1]
    half = grad_attended.shape[0]
    members = half // SEQ
    grad_attended[...] = dot_nt(grad_ref[start : start + half, :].astype(BF16), output_ref[...]).astype(BF16)
    held = {}
    for turn in range(members + 1):
        if turn < members:
            member = start // SEQ + turn
            tokens = slice(start + turn * SEQ, start + (turn + 1) * SEQ)
            here = slice(turn * SEQ, (turn + 1) * SEQ)
            for pair in range(PAIRS):
                _, lanes, columns = unit_of(pair)
                turned = grad_attended[here, lanes].astype(F32).T * feature_scale(inverse_ref[member, :, columns])
                inner_sum = feature_sums(turned * blend_ref[member, lanes, :].astype(F32))
                grad_rows = head_pair_rows(turned.T.astype(BF16))
                held[turn, pair] = (inner_sum, grad_rows, dot_nt(values_ref[tokens, lanes], grad_rows))
        if turn:
            member = start // SEQ + turn - 1
            tokens = slice(start + (turn - 1) * SEQ, start + turn * SEQ)
            for pair in range(PAIRS):
                _, lanes, columns = unit_of(pair)
                inner_sum, grad_rows, grad_powered = held.pop((turn - 1, pair))
                powered = powered_ref[member, :, columns]
                grad_scores = (powered.astype(F32) * (grad_powered - inner_sum)).astype(BF16)
                pulled = (
                    head_pair_diagonal(dot_tn(keys_ref[tokens, lanes], grad_scores), SEQ).T,
                    dot_nn(grad_scores, head_pair_rows(queries_ref[tokens, lanes])),
                    dot_nn(powered, grad_rows),
                )
                for at, piece in enumerate(pulled):
                    left = at * width + pair * PAIR
                    pulled_ref[tokens, left : left + PAIR] = piece.astype(BF16)
    if last_piece:
        rows = input_ref[...].astype(F32)
        normed = (rows * inverse_rms(rows) * gain_ref[...]).astype(BF16)
        for at in range(3):
            lanes = slice(at * width, (at + 1) * width)
            staged[:, lanes] = dot_tn(normed, pulled_ref[:, lanes]).astype(BF16)
        store_wide(codes_ref[0], staged, keep_ref, send_ref)


def self_backward(
    codes, former, grad_after, queries, keys, values, powered, inverse, blend, self_output, inputs, self_gain
):
    tokens, width = inputs.shape
    half = tokens // 2
    last_piece = former is not None
    operands = (codes, grad_after, queries, keys, values, powered, inverse, blend, self_output)
    scratch = [pltpu.VMEM((half, width), BF16)]
    if last_piece:
        outs = [near((tokens, 3 * width), BF16)] + [near((1, width // 2, 3 * width), BF16)] * 2
        operands += (former, inputs, self_gain)
        scratch = [pltpu.VMEM((width, 3 * width), BF16)] + scratch
    else:
        outs = [near((half, 3 * width), BF16)]
    return resident(
        functools.partial(self_pull_body, last_piece), "self_backward", operands, outs, scratch, scalars=1, vmem=24, cost=6
    )


def self_close_body(pulled_ref, grad_ref, input_ref, gain_ref, query_ref, key_ref, value_ref, grad_inputs_ref):
    width = input_ref.shape[1]
    block = grad_inputs_ref.shape[0]
    here = pl.ds(pl.multiple_of(pl.program_id(0) * block, block), block)
    rows = input_ref[here, :].astype(F32)
    grad_normed = (
        dot_nt(pulled_ref[here, :width], query_ref[...])
        + dot_nt(pulled_ref[here, width : 2 * width], key_ref[...])
        + dot_nt(pulled_ref[here, 2 * width :], value_ref[...])
    )
    grad_inputs_ref[...] = grad_ref[here, :] + norm_pull(rows, inverse_rms(rows), gain_ref[...], grad_normed)


def self_close(pulled, grad_after, inputs, self_gain, self_query, self_key, self_value):
    tokens, width = inputs.shape
    block = 256 if tokens % 256 == 0 else tokens
    whole = pl.BlockSpec(memory_space=pltpu.VMEM)
    return call(
        self_close_body, "self_close", (tokens // block,), [whole] * 7,
        pl.BlockSpec((block, width), lambda i: (i, 0)), far((tokens, width), F32), vmem=14, cost=3,
    )(pulled, grad_after, inputs, self_gain, self_query, self_key, self_value)


CHUNK = 256


def unit_of(unit):
    pair = unit % PAIRS
    return unit // PAIRS, slice(pair * PAIR, (pair + 1) * PAIR), slice(pair * 2 * SEQ, (pair + 1) * 2 * SEQ)


def fold_rows(values, operation):
    return operation(values.reshape(values.shape[0] // 8, 8, values.shape[1]), axis=0)


def cross_body(
    per_step, shared, chosen_ref, queries_ref, keys_ref, values_t_ref, ids_ref,
    powered_ref, inverse_ref, blend_ref, attended_ref, held,
):
    step = pl.program_id(0)
    slots = keys_ref.shape[1]
    chunks = [slice(start, start + CHUNK) for start in range(0, slots, CHUNK)]
    biases = []
    for member in range(per_step):
        ids = ids_ref[0 if shared else member]
        at = step * per_step + member
        seen = ids == chosen_ref[at, 0]
        for place in range(1, chosen_ref.shape[1]):
            seen = seen | (ids == chosen_ref[at, place])
        biases.append(jnp.where(seen, 0.0, MASKED).astype(F32))
    units = per_step * PAIRS
    queries, largest, totals, inverses = {}, {}, {}, {}
    for turn in range(units + 2):
        for at, rows in enumerate(chunks):
            unit = turn
            if unit < units:
                member, lanes, columns = unit_of(unit)
                pool = 0 if shared else member
                if at == 0:
                    queries[unit] = head_pair_rows(queries_ref[member * SEQ : (member + 1) * SEQ, lanes])
                bias = biases[member][rows]
                scores = dot_nt(keys_ref[pool, rows, lanes], queries[unit])
                scores = scores + jnp.concatenate([bias, bias], axis=1)
                held[unit % 2, rows, :] = scores
                high = fold_rows(scores, jnp.max)
                largest[unit] = high if at == 0 else jnp.maximum(largest[unit], high)
                if at == len(chunks) - 1:
                    largest[unit] = jnp.max(largest[unit], axis=0, keepdims=True)
            unit = turn - 1
            if 0 <= unit < units:
                member, lanes, columns = unit_of(unit)
                powered = jnp.exp(held[unit % 2, rows, :] - largest[unit])
                total = fold_rows(powered, jnp.sum)
                totals[unit] = total if at == 0 else totals[unit] + total
                powered_ref[member, rows, columns] = powered.astype(BF16)
                if at == len(chunks) - 1:
                    inverses[unit] = 1.0 / jnp.sum(totals[unit], axis=0, keepdims=True)
                    inverse_ref[member, :, columns] = inverses[unit]
            unit = turn - 2
            if 0 <= unit < units and at == len(chunks) - 1:
                member, lanes, columns = unit_of(unit)
                pool = 0 if shared else member
                blend = dot_nn(values_t_ref[pool, lanes, :], powered_ref[member, :, columns])
                blend = head_pair_diagonal(blend * inverses[unit], SEQ)
                blend_ref[member, lanes, :] = blend.astype(BF16)
                attended_ref[member * SEQ : (member + 1) * SEQ, lanes] = blend.T.astype(BF16)


def cross_whole_body(
    chosen_ref, queries_ref, keys_ref, values_t_ref, ids_ref, *refs
):
    powered_refs = refs[:PAIRS]
    inverse_ref, blend_ref, attended_ref, held = refs[PAIRS:]
    slots = keys_ref.shape[1]
    chunks = [slice(start, start + CHUNK) for start in range(0, slots, CHUNK)]
    per_step = 2
    units = per_step * PAIRS

    def some(step, carry):
        biases = []
        for inner in range(per_step):
            at = step * per_step + inner
            seen = ids_ref[0] == chosen_ref[at, 0]
            for place in range(1, chosen_ref.shape[1]):
                seen = seen | (ids_ref[0] == chosen_ref[at, place])
            biases.append(jnp.where(seen, 0.0, MASKED).astype(F32))
        queries, largest, totals, inverses = {}, {}, {}, {}
        for turn in range(units + 2):
            for at, rows in enumerate(chunks):
                unit = turn
                if unit < units:
                    inner, lanes, columns = unit_of(unit)
                    member = step * per_step + inner
                    tokens = pl.ds(pl.multiple_of(member * SEQ, SEQ), SEQ)
                    if at == 0:
                        queries[unit] = head_pair_rows(queries_ref[tokens, lanes])
                    bias = biases[inner][rows]
                    scores = dot_nt(keys_ref[0, rows, lanes], queries[unit])
                    scores = scores + jnp.concatenate([bias, bias], axis=1)
                    held[unit % 2, rows, :] = scores
                    high = fold_rows(scores, jnp.max)
                    largest[unit] = high if at == 0 else jnp.maximum(largest[unit], high)
                    if at == len(chunks) - 1:
                        largest[unit] = jnp.max(largest[unit], axis=0, keepdims=True)
                unit = turn - 1
                if 0 <= unit < units:
                    inner, lanes, columns = unit_of(unit)
                    member = step * per_step + inner
                    powered = jnp.exp(held[unit % 2, rows, :] - largest[unit])
                    total = fold_rows(powered, jnp.sum)
                    totals[unit] = total if at == 0 else totals[unit] + total
                    powered_refs[unit % PAIRS][member, rows, :] = powered.astype(BF16)
                    if at == len(chunks) - 1:
                        inverses[unit] = 1.0 / jnp.sum(totals[unit], axis=0, keepdims=True)
                        inverse_ref[member, :, columns] = inverses[unit]
                unit = turn - 2
                if 0 <= unit < units and at == len(chunks) - 1:
                    inner, lanes, columns = unit_of(unit)
                    member = step * per_step + inner
                    tokens = pl.ds(pl.multiple_of(member * SEQ, SEQ), SEQ)
                    blend = dot_nn(values_t_ref[0, lanes, :], powered_refs[unit % PAIRS][member])
                    blend = head_pair_diagonal(blend * inverses[unit], SEQ)
                    blend_ref[member, lanes, :] = blend.astype(BF16)
                    attended_ref[tokens, lanes] = blend.T.astype(BF16)
        return carry

    lax.fori_loop(0, queries_ref.shape[0] // SEQ // per_step, some, 0)


def cross_forward(chosen, queries, keys, values_t, ids):
    tokens, width = queries.shape
    queries_here = tokens // SEQ
    slots = keys.shape[1]
    if keys.shape[0] > 1:
        return cross_forward_slots(chosen, queries, keys, values_t, ids)
    *powered, inverse, blend, attended = resident(
        cross_whole_body,
        "cross_forward",
        (chosen, queries, keys, values_t, ids),
        [near((queries_here, slots, 2 * SEQ), BF16)] * PAIRS
        + [
            near((queries_here, 1, HEADS * SEQ), F32),
            near((queries_here, width, SEQ), BF16),
            near((tokens, width), BF16),
        ],
        [pltpu.VMEM((2, slots, 2 * SEQ), F32)],
        scalars=1, vmem=14, cost=15,
    )
    return powered, inverse, blend, attended


def cross_forward_slots(chosen, queries, keys, values_t, ids):
    tokens, width = queries.shape
    queries_here = tokens // SEQ
    shared = keys.shape[0] == 1
    slots = keys.shape[1]
    columns = HEADS * SEQ
    per_step = 2 if shared else 1

    def pool_spec(*shape):
        return fixed((1,) + shape) if shared else pl.BlockSpec((per_step,) + shape, lambda i, *_: (i, 0, 0))

    def query_spec(*shape):
        return pl.BlockSpec((per_step,) + shape, lambda i, *_: (i, 0, 0))

    row_spec = pl.BlockSpec((per_step * SEQ, width), lambda i, *_: (i, 0))
    return functools.partial(call, cost=20, vmem=26)(
        functools.partial(cross_body, per_step, shared),
        "cross_forward",
        (queries_here // per_step,),
        [row_spec, pool_spec(slots, width), pool_spec(width, slots), pool_spec(slots, SEQ)],
        [query_spec(slots, columns), query_spec(1, columns), query_spec(width, SEQ), row_spec],
        [
            far((queries_here, slots, columns), BF16),
            near((queries_here, 1, columns), F32),
            near((queries_here, width, SEQ), BF16),
            near((tokens, width), BF16),
        ],
        [pltpu.VMEM((2, slots, 2 * SEQ), F32)],
        prefetch=1,
    )(chosen, queries, keys, values_t, ids)


def feature_scale(inverse):
    return jnp.concatenate(
        [jnp.broadcast_to(inverse[:, :SEQ], (HDIM, SEQ)), jnp.broadcast_to(inverse[:, SEQ:], (HDIM, SEQ))], axis=0
    )


def feature_sums(values):
    return jnp.concatenate(
        [jnp.sum(values[:HDIM], axis=0, keepdims=True), jnp.sum(values[HDIM:], axis=0, keepdims=True)], axis=1
    )


def cross_pull_body(
    per_step, shared, grad_ref, queries_ref, keys_t_ref, values_ref, powered_ref, inverse_ref, blend_ref,
    pulled_ref, grad_keys_ref, grad_values_ref, held, keys_sum, values_sum,
):
    step = pl.program_id(0)
    last = pl.num_programs(0) - 1
    members = range(per_step)
    stack = per_step if shared else 1
    chunks = [slice(start, start + CHUNK) for start in range(0, values_ref.shape[1], CHUNK)]

    @pl.when(step == 0)
    def _():
        keys_sum[...] = jnp.zeros_like(keys_sum)
        values_sum[...] = jnp.zeros_like(values_sum)

    grads, sums, queries = [], [], []
    for member in members:
        tokens = slice(member * SEQ, (member + 1) * SEQ)
        turned = grad_ref[tokens, :].astype(F32).T * feature_scale(inverse_ref[member])
        sums.append(feature_sums(turned * blend_ref[member].astype(F32)))
        grads.append(head_pair_rows(turned.T.astype(BF16)))
        queries.append(head_pair_rows(queries_ref[tokens, :]))
    grads = jnp.concatenate(grads, axis=0)
    queries = jnp.concatenate(queries, axis=0)
    sums = jnp.concatenate(sums, axis=1)
    grad_powered = {}
    for at in range(len(chunks) + 1):
        if at < len(chunks):
            grad_powered[at] = dot_nt(values_ref[0, chunks[at], :], grads)
        if at:
            rows = chunks[at - 1]
            powered = jnp.concatenate([powered_ref[member, rows, :] for member in members], axis=1)
            held[rows, :] = (powered.astype(F32) * (grad_powered.pop(at - 1) - sums)).astype(BF16)
            values_sum[rows, :] += dot_nn(powered, grads)
            keys_sum[rows, :] += dot_nn(held[rows, :], queries)
    pulled = dot_nn(keys_t_ref[0], held[...])
    for member in members:
        mine = pulled[:, member * 2 * SEQ : (member + 1) * 2 * SEQ]
        pulled_ref[member * SEQ : (member + 1) * SEQ, :] = head_pair_diagonal(mine, SEQ).T.astype(BF16)
    if shared:

        @pl.when(step == last)
        def _():
            grad_keys_ref[0] = keys_sum[...].astype(grad_keys_ref.dtype)
            grad_values_ref[0] = values_sum[...].astype(grad_values_ref.dtype)

    else:
        grad_keys_ref[0] = keys_sum[...].astype(grad_keys_ref.dtype)
        grad_values_ref[0] = values_sum[...].astype(grad_values_ref.dtype)
        keys_sum[...] = jnp.zeros_like(keys_sum)
        values_sum[...] = jnp.zeros_like(values_sum)


def cross_pull_whole_body(
    pair, grad_ref, queries_ref, keys_t_ref, values_ref, powered_ref, inverse_ref, blend_ref,
    pulled_ref, grad_keys_ref, grad_values_ref, held, keys_sum, values_sum,
):
    _, lanes, columns = unit_of(pair)
    slots = values_ref.shape[1]
    chunks = [slice(start, start + CHUNK) for start in range(0, slots, CHUNK)]
    count = grad_ref.shape[0] // SEQ
    per_step = 2
    for first in range(0, count, per_step):
        members = range(first, first + per_step)
        grads, sums, queries = [], [], []
        for member in members:
            tokens = slice(member * SEQ, (member + 1) * SEQ)
            turned = grad_ref[tokens, lanes].astype(F32).T * feature_scale(inverse_ref[member, :, columns])
            sums.append(feature_sums(turned * blend_ref[member, lanes, :].astype(F32)))
            grads.append(head_pair_rows(turned.T.astype(BF16)))
            queries.append(head_pair_rows(queries_ref[tokens, lanes]))
        grads = jnp.concatenate(grads, axis=0)
        queries = jnp.concatenate(queries, axis=0)
        sums = jnp.concatenate(sums, axis=1)
        powered, grad_powered = {}, {}
        for at in range(len(chunks) + 1):
            if at < len(chunks):
                rows = chunks[at]
                grad_powered[at] = dot_nt(values_ref[0, rows, lanes], grads)
                powered[at] = jnp.concatenate([powered_ref[member, rows, :] for member in members], axis=1)
                term = dot_nn(powered[at], grads)
                values_sum[rows, :] = values_sum[rows, :] + term if first else term
            if at:
                rows = chunks[at - 1]
                held[rows, :] = (powered.pop(at - 1).astype(F32) * (grad_powered.pop(at - 1) - sums)).astype(BF16)
                term = dot_nn(held[rows, :], queries)
                keys_sum[rows, :] = keys_sum[rows, :] + term if first else term
        pulled = dot_nn(keys_t_ref[0, lanes, :], held[...])
        for at, member in enumerate(members):
            mine = pulled[:, at * 2 * SEQ : (at + 1) * 2 * SEQ]
            pulled_ref[member * SEQ : (member + 1) * SEQ, :] = head_pair_diagonal(mine, SEQ).T.astype(BF16)
    grad_keys_ref[0] = keys_sum[...].astype(BF16)
    grad_values_ref[0] = values_sum[...].astype(BF16)


def cross_backward(pair, grad_attended, queries, keys_t, values, powered, inverse, blend):
    tokens, slots = queries.shape[0], values.shape[1]
    if values.shape[0] > 1:
        return cross_backward_slots(pair, grad_attended, queries, keys_t, values, powered, inverse, blend)
    return resident(
        functools.partial(cross_pull_whole_body, pair),
        "cross_backward",
        (grad_attended, queries, keys_t, values, powered[pair], inverse, blend),
        [near((tokens, PAIR), BF16)] + [near((1, slots, PAIR), BF16)] * 2,
        [pltpu.VMEM((slots, 4 * SEQ), BF16), pltpu.VMEM((slots, PAIR), F32), pltpu.VMEM((slots, PAIR), F32)],
        vmem=14, cost=4,
    )


def cross_backward_slots(pair, grad_attended, queries, keys_t, values, powered, inverse, blend):
    tokens, width = queries.shape
    queries_here = tokens // SEQ
    pools, slots = values.shape[:2]
    shared = pools == 1
    per_step = 2 if shared else 1

    def pool_index(column):
        if shared:
            return lambda i: (0, pair, 0) if column else (0, 0, pair)
        return lambda i: (i, pair, 0) if column else (i, 0, pair)

    row_spec = pl.BlockSpec((per_step * SEQ, PAIR), lambda i: (i, pair))
    slot_spec = pl.BlockSpec((1, slots, PAIR), (lambda i: (0, 0, 0)) if shared else (lambda i: (i, 0, 0)))
    dtype = BF16 if shared else F32
    return functools.partial(call, vmem=14)(
        functools.partial(cross_pull_body, per_step, shared),
        "cross_backward",
        (queries_here // per_step,),
        [
            row_spec, row_spec,
            pl.BlockSpec((1, PAIR, slots), pool_index(True)), pl.BlockSpec((1, slots, PAIR), pool_index(False)),
            pl.BlockSpec((per_step, slots, 2 * SEQ), lambda i: (i, 0, pair)),
            pl.BlockSpec((per_step, 1, 2 * SEQ), lambda i: (i, 0, pair)),
            pl.BlockSpec((per_step, PAIR, SEQ), lambda i: (i, pair, 0)),
        ],
        [pl.BlockSpec((per_step * SEQ, PAIR), lambda i: (i, 0)), slot_spec, slot_spec],
        [far((tokens, PAIR), BF16)] + [far((pools, slots, PAIR), dtype)] * 2,
        [
            pltpu.VMEM((slots, per_step * 2 * SEQ), BF16),
            pltpu.VMEM((slots, PAIR), F32), pltpu.VMEM((slots, PAIR), F32),
        ],
        cost=7,
    )(grad_attended, queries, keys_t, values, streamed(powered), inverse, blend)


def cross_close_body(
    codes_ref, pulled_0, pulled_1, pulled_2, pulled_3, after_ref, grad_cross_ref, gain_ref, query_ref, attended_ref,
    grad_after_ref, keep_ref, send_ref, staged,
):
    rows = after_ref[...]
    scale = inverse_rms(rows)
    normed = (rows * scale * gain_ref[...]).astype(BF16)
    pulled = jnp.concatenate([pulled_0[...], pulled_1[...], pulled_2[...], pulled_3[...]], axis=1)
    store_turned(codes_ref[0], dot_tn(normed, pulled), keep_ref, send_ref, 0, staged)
    grad_after = grad_cross_ref[...] + norm_pull(rows, scale, gain_ref[...], dot_nt(pulled, query_ref[...]))
    grad_after_ref[...] = grad_after
    grad_output = dot_tn(attended_ref[...], grad_after.astype(BF16))
    store_turned(codes_ref[0], grad_output, keep_ref, send_ref, 1, staged)


def cross_close(codes, pulled, after_self, grad_after_cross, cross_gain, cross_query, self_attended):
    tokens, width = after_self.shape
    return resident(
        cross_close_body,
        "cross_close",
        (codes, *pulled, after_self, grad_after_cross, cross_gain, cross_query, self_attended),
        [near((tokens, width), F32)] + [near((2, width // 2, width), BF16)] * 2,
        [pltpu.VMEM((width, width), BF16)],
        scalars=1, cost=3,
    )


TANH_SLOPE = 0.7978845608028654
TANH_CUBE = 0.044715


def feed_body(
    limits_ref, codes_ref, after_ref, attended_ref, cotangent_ref, gain_ref, output_ref, inner_ref, outer_ref,
    layer_ref, grad_after_ref, grad_attended_ref, keep_a, send_a, keep_b, send_b,
    after_cross, normed, grad_feed, total, grad_normed, hidden, grad_pre, staged,
):
    tokens, width = after_cross.shape
    steps = inner_ref.shape[1] // width
    spans = [slice(start, start + 256) for start in range(0, tokens, 256)]
    place = lax.broadcasted_iota(jnp.int32, (SEQ, width), 0)
    for member in range(tokens // SEQ):
        span = slice(member * SEQ, (member + 1) * SEQ)
        grads = cotangent_ref[span, :]
        grad_feed[span, :] = jnp.where(place < limits_ref[member], grads, jnp.zeros_like(grads))
    for span in spans:
        rows = after_ref[span, :] + dot_nn(attended_ref[span, :], output_ref[...])
        after_cross[span, :] = rows
        normed[span, :] = (rows * inverse_rms(rows) * gain_ref[...]).astype(BF16)
    for step in range(steps):
        here = slice(step * width, (step + 1) * width)
        inner, outer = inner_ref[:, here], outer_ref[here, :]
        made = {}
        for turn in range(len(spans) + 1):
            if turn < len(spans):
                span = spans[turn]
                made[turn] = (dot_nn(normed[span, :], inner), dot_nt(grad_feed[span, :], outer))
            if turn:
                span = spans[turn - 1]
                pre, grad_hidden = made.pop(turn - 1)
                squared = pre * pre
                half = 0.5 * jnp.tanh(pre * (TANH_SLOPE + (TANH_SLOPE * TANH_CUBE) * squared)) + 0.5
                unit = (pre * half).astype(BF16)
                slope = half + (pre * (2.0 * half * (1.0 - half))) * (
                    TANH_SLOPE + (3.0 * TANH_SLOPE * TANH_CUBE) * squared
                )
                pulled = (grad_hidden * slope).astype(BF16)
                hidden[span, :] = unit
                grad_pre[span, :] = pulled
                term = dot_nn(unit, outer)
                total[span, :] = total[span, :] + term if step else after_cross[span, :] + term
                term = dot_nt(pulled, inner)
                grad_normed[span, :] = grad_normed[span, :] + term if step else term
        store_turned(codes_ref[0], dot_tn(hidden[...], grad_feed[...]), keep_a, send_a, step, staged)
        store_turned(codes_ref[1], dot_tn(normed[...], grad_pre[...]), keep_b, send_b, step, staged)
    for span in spans:
        layer_ref[span, :] = total[span, :].astype(BF16)
        rows = after_cross[span, :]
        grad_rows = norm_pull(rows, inverse_rms(rows), gain_ref[...], grad_normed[span, :])
        grad_after = grad_feed[span, :].astype(F32) + grad_rows
        grad_after_ref[span, :] = grad_after
        hidden[span, :] = grad_after.astype(BF16)
        grad_attended_ref[span, :] = dot_nt(hidden[span, :], output_ref[...]).astype(BF16)
    store_turned(codes_ref[0], dot_tn(attended_ref[...], hidden[...]), keep_a, send_a, steps, staged)


def feed_both(limits, codes, after_self, attended, cotangent, feed_gain, cross_output, inner_weight, outer_weight):
    tokens, width = after_self.shape
    count = inner_weight.shape[1] // width
    return resident(
        feed_body,
        "feed_both",
        (limits, codes, after_self, attended, cotangent, feed_gain, cross_output, inner_weight, outer_weight),
        [near((tokens, width), BF16), near((tokens, width), F32), near((tokens, width), BF16)]
        + [near((count + 1, width // 2, width), BF16)] * 2 + [near((count, width // 2, width), BF16)] * 2,
        [
            pltpu.VMEM((tokens, width), F32), pltpu.VMEM((tokens, width), BF16), pltpu.VMEM((tokens, width), BF16),
            pltpu.VMEM((tokens, width), F32), pltpu.VMEM((tokens, width), F32),
            pltpu.VMEM((tokens, width), BF16), pltpu.VMEM((tokens, width), BF16), pltpu.VMEM((width, width), BF16),
        ],
        scalars=2, vmem=24, cost=18,
    )


def permute(values, batch_bits, mem_bits):
    if batch_bits and mem_bits:
        batch, mem = lax.axis_size("batch"), lax.axis_size("mem")
        pairs = [(i * mem + j, (i ^ batch_bits) * mem + (j ^ mem_bits)) for i in range(batch) for j in range(mem)]
        return lax.ppermute(values, ("batch", "mem"), pairs)
    if batch_bits:
        axis, bits, count = "batch", batch_bits, lax.axis_size("batch")
    else:
        axis, bits, count = "mem", mem_bits, lax.axis_size("mem")
    return lax.ppermute(values, axis, [(at, at ^ bits) for at in range(count)])


CORE, ACROSS, ALONG, BOTH = (1, 0), (2, 0), (0, 1), (2, 1)
DEEP = ((0, 2), (0, 4), (0, 6))
NEAR, DISTANT = DEEP[:2]


def added(*terms):
    total = terms[0].astype(F32)
    for term in terms[1:]:
        total = total + term.astype(F32)
    return total.astype(BF16)


def portions(count, *terms):
    size = terms[0].shape[1] // count
    return [added(*[t[:, i * size : (i + 1) * size] for t in terms]) for i in range(count)]


def beyond(values):
    bits = 8
    while bits < lax.axis_size("mem"):
        values = added(values, permute(values, 0, bits))
        bits *= 2
    return values


def reduce_part(keep_a, send_a, keep_b, send_b):
    keep_a, keep_b, got_a, got_b = yield (keep_a, keep_b, permute(send_a, *CORE), permute(send_b, *CORE))
    keep_a, send_a = portions(2, keep_a, got_a)
    keep_b, send_b = portions(2, keep_b, got_b)
    keep_a, keep_b, got_a, got_b = yield (keep_a, keep_b, permute(send_a, *ACROSS), permute(send_b, *ALONG))
    keep_a, send_a = portions(2, keep_a, got_a)
    keep_b, send_b = portions(2, keep_b, got_b)
    keep_a, keep_b, got_a, got_b = yield (keep_a, keep_b, permute(send_a, *ALONG), permute(send_b, *ACROSS))
    pairs = zip(portions(2, keep_a, got_a), portions(2, keep_b, got_b))
    keep, send = [jnp.concatenate(pair, axis=0) for pair in pairs]
    keep, got = yield (keep, permute(send, *NEAR))
    keep, send = portions(2, keep, got)
    keep, got = yield (keep, permute(send, *DISTANT))
    yield (beyond(added(keep, got)),)


def reduce_direct(keep, send):
    keep, got = yield (keep, permute(send, *CORE))
    parts = portions(4, keep, got)
    got = yield (parts[0], permute(parts[1], *ALONG), permute(parts[2], *ACROSS), permute(parts[3], *BOTH))
    keep, send = portions(2, *got)
    keep, got = yield (keep, permute(send, *NEAR))
    keep, send = portions(2, keep, got)
    keep, got = yield (keep, permute(send, *DISTANT))
    whole = beyond(added(keep, got))
    for bits in (DISTANT, NEAR):
        got = yield (whole, permute(whole, *bits))
        whole = jnp.concatenate(got, axis=1)
    got = yield (whole, permute(whole, *ALONG), permute(whole, *ACROSS), permute(whole, *BOTH))
    whole = jnp.concatenate(got, axis=1)
    yield (whole, permute(whole, *CORE))


class Sum:
    def __init__(self, *arrays):
        part = len(arrays) == 4
        self.steps = reduce_part(*arrays) if part else reduce_direct(*arrays)
        self.arrays = next(self.steps)
        self.left = 5 if part else 7


def advance(sums, done):
    open_sums = [member for member in sums if member.left >= 0]
    flat = sum([tuple(member.arrays) for member in open_sums], ())
    tied = lax.optimization_barrier(flat + tuple(done))
    for member in open_sums:
        size = len(member.arrays)
        mine, tied = tied[:size], tied[size:]
        member.arrays = member.steps.send(mine) if member.left else mine
        member.left -= 1
    kept = lax.optimization_barrier(tuple(member.arrays[0] for member in open_sums) + tuple(tied))
    for member, first in zip(open_sums, kept):
        member.arrays = (first,) + tuple(member.arrays[1:])
    return kept[len(open_sums) :]


def follow(member, *others):
    size = len(member.arrays)
    tied = lax.optimization_barrier(tuple(member.arrays) + tuple(other.arrays[0] for other in others))
    for other, kept in zip(others, tied[size:]):
        other.arrays = (kept,) + tuple(other.arrays[1:])
    member.arrays = member.steps.send(tied[:size]) if member.left else tied[:size]
    member.left -= 1


def restore(code, own, other, at, target, rows):
    size = 2 * own.shape[1] // BLOCKS
    half = BLOCKS // 2
    for place in range(BLOCKS):
        source = own if place < half else other
        start = (place % half) * size
        goal = pl.ds(pl.multiple_of((place ^ code) * size + rows, size), size)
        target[goal, :] = source[at, start : start + size, :].astype(F32)


def fold_lanes(values):
    total = values[:, :128]
    for start in range(128, values.shape[1], 128):
        total = total + values[:, start : start + 128]
    return total


def owner_of(place, along_first):
    core, high, low, deep = place >> 4, (place >> 3) & 1, (place >> 2) & 1, place & 3
    across, along = (low, high) if along_first else (high, low)
    return across * 2 + core, (deep & 2) | ((deep & 1) << 2) | along


def settle(source, target, along_first):
    size = source.shape[3]
    for place in range(BLOCKS):
        batch_at, mem_at = owner_of(place, along_first)
        target[place * size : (place + 1) * size, :] = source[batch_at, mem_at, 0].astype(F32)


def restore_rows_body(source, out_ref):
    settle(source, out_ref, False)


def gathered_spec(gathered, first):
    size, width = gathered.shape[3:]
    return pl.BlockSpec((gathered.shape[0], 8, 1, size, width), lambda i: (0, 0, first + i, 0, 0))


def restore_rows(gathered, first, count):
    size, width = gathered.shape[3:]
    rows = BLOCKS * size
    return call(
        restore_rows_body, "restore_rows", (count,), [gathered_spec(gathered, first)],
        pl.BlockSpec((rows, width), lambda i: (i, 0)), shaped((count * rows, width), F32), vmem=10,
    )(gathered)


def restore_columns_body(source, weight_ref, gain_ref, out_ref, grad_gain_ref, sums):
    step = pl.program_id(0)

    @pl.when(step == 0)
    def _():
        sums[...] = jnp.zeros_like(sums)

    settle(source, out_ref, True)
    sums[...] += fold_lanes(out_ref[...] * weight_ref[...].astype(F32))

    @pl.when(step == pl.num_programs(0) - 1)
    def _():
        grad_gain_ref[...] = jnp.sum(sums[...].T, axis=0, keepdims=True) / gain_ref[...]


def restore_columns(gathered, first, count, weight, gain):
    size, width = gathered.shape[3:]
    rows = BLOCKS * size
    wide = pl.BlockSpec((rows, width), lambda i: (0, i))
    return call(
        restore_columns_body, "restore_columns", (count,), [gathered_spec(gathered, first), wide, fixed((1, rows))],
        [wide, fixed((1, rows))],
        [shaped((rows, count * width), F32), shaped((1, rows), F32)],
        [pltpu.VMEM((rows, 128), F32)], vmem=12,
    )(gathered, streamed(weight), gain)


def restore_cross_body(
    codes_ref, own_ref, other_ref, query_ref, key_ref, value_ref, cross_gain_ref, encoder_gain_ref,
    query_out, self_out, key_out, value_out, cross_gain_out, encoder_gain_out,
):
    for at, target in enumerate((query_out, self_out, key_out, value_out)):
        restore(codes_ref[0], own_ref, other_ref, at, target, 0)
    sums = fold_lanes(query_out[...] * query_ref[...].astype(F32))
    cross_gain_out[...] = jnp.sum(sums.T, axis=0, keepdims=True) / cross_gain_ref[...]
    sums = fold_lanes(
        key_out[...] * key_ref[...].astype(F32) + value_out[...] * value_ref[...].astype(F32)
    )
    encoder_gain_out[...] = jnp.sum(sums.T, axis=0, keepdims=True) / encoder_gain_ref[...]


def restore_cross(codes, own, other, cross_query, cross_key, cross_value, cross_gain, encoder_gain):
    width = own.shape[2]
    weight, row = fixed((width, width)), fixed((1, width))
    return call(
        restore_cross_body, "restore_cross", (1,),
        [fixed(own.shape)] * 2 + [weight] * 3 + [row] * 2,
        [weight] * 4 + [row] * 2,
        [shaped((width, width), F32)] * 4 + [shaped((1, width), F32)] * 2, prefetch=1, vmem=16,
    )(codes, own, other, *map(streamed, (cross_query, cross_key, cross_value)), cross_gain, encoder_gain)


def restore_self_body(
    codes_ref, own_ref, other_ref, query_ref, key_ref, value_ref, gain_ref, query_out, key_out, value_out, gain_out
):
    half = BLOCKS // 2
    width = query_out.shape[1]
    size = query_out.shape[0] // BLOCKS
    for place in range(BLOCKS):
        start = slice((place % half) * size, (place % half + 1) * size)
        source = own_ref if place < half else other_ref
        goal = pl.ds(pl.multiple_of((place ^ codes_ref[0]) * size, size), size)
        query_out[goal, :] = source[0, start, :width].astype(F32)
        key_out[goal, :] = source[0, start, width : 2 * width].astype(F32)
        value_out[goal, :] = source[0, start, 2 * width :].astype(F32)
    sums = fold_lanes(
        query_out[...] * query_ref[...].astype(F32)
        + key_out[...] * key_ref[...].astype(F32)
        + value_out[...] * value_ref[...].astype(F32)
    )
    gain_out[...] = jnp.sum(sums.T, axis=0, keepdims=True) / gain_ref[...]


def restore_self(codes, own, other, self_query, self_key, self_value, self_gain):
    width = self_query.shape[0]
    weight, row = fixed((width, width)), fixed((1, width))
    return call(
        restore_self_body, "restore_self", (1,),
        [fixed(own.shape)] * 2 + [weight] * 3 + [row],
        [weight] * 3 + [row],
        [shaped((width, width), F32)] * 3 + [shaped((1, width), F32)], prefetch=1, vmem=16,
    )(codes, own, other, *map(streamed, (self_query, self_key, self_value)), self_gain)


def device_codes(shared):
    batch_at, mem_at = lax.axis_index("batch"), lax.axis_index("mem")
    core, across = batch_at & 1, batch_at >> 1
    along, deep = mem_at & 1, (mem_at & 2) | ((mem_at >> 2) & 1)
    return jnp.stack(
        [
            (core << 4) | (across << 3) | (along << 2) | deep,
            (core << 4) | (along << 3) | (across << 2) | deep,
            mem_at if shared else jnp.zeros_like(mem_at),
        ]
    ).astype(jnp.int32)


def passage_slots(pool_ids, chosen, passages, pool_rows):
    passage_marks = jnp.arange(passages, dtype=jnp.int32)
    starts = jnp.sum(
        (pool_ids[None, :] < passage_marks[:, None]).astype(jnp.int32), axis=1, dtype=jnp.int32
    )
    counts = jnp.sum(
        (pool_ids[None, :] == passage_marks[:, None]).astype(jnp.int32), axis=1, dtype=jnp.int32
    )
    picked = (chosen[..., None] == passage_marks).astype(jnp.int32)
    first_row = jnp.sum(picked * starts, axis=-1, dtype=jnp.int32)
    extent = jnp.sum(picked * counts, axis=-1, dtype=jnp.int32)
    offsets = jnp.arange(PLEN, dtype=jnp.int32)
    slot_rows = jnp.minimum(first_row[..., None] + offsets, pool_rows - 1)
    slot_visible = offsets < extent[..., None]
    slot_shape = (chosen.shape[0], chosen.shape[1] * PLEN)
    return (slot_rows.reshape(slot_shape), slot_visible.reshape(slot_shape))


def local(
    inputs,
    cotangent,
    memory,
    passage_ids,
    retrieved,
    task_ids,
    target_lens,
    encoder_gain,
    self_gain,
    cross_gain,
    feed_gain,
    self_query,
    self_key,
    self_value,
    self_output,
    cross_query,
    cross_key,
    cross_value,
    cross_output,
    inner_weight,
    outer_weight,
):
    width = inputs.shape[2]
    own_rows = memory.shape[1]
    chosen = retrieved[0]
    devices = lax.axis_size("mem")
    pool_rows = own_rows * devices
    slots = chosen.shape[1] * PLEN
    shared = pool_rows <= slots
    codes = device_codes(shared)
    encoder_row, self_row, cross_row, feed_row = (
        member.reshape(1, width) for member in (encoder_gain, self_gain, cross_gain, feed_gain)
    )
    id_rows = jnp.zeros((8, width), BF16).at[0, :own_rows].set(passage_ids[0].astype(BF16))
    own_block = jnp.concatenate([memory[0], id_rows], axis=0)
    line = [own_block] + [permute(own_block, *bits) for bits in DEEP]
    beside = permute(own_block, *ALONG)
    opened = self_open(inputs[0], self_row, self_query, self_key, self_value)
    tied = lax.optimization_barrier((*line, beside, *opened))
    line, beside, opened = list(tied[: len(line)]), tied[len(line)], tied[len(line) + 1 :]
    line_beside = [beside] + [permute(member, *ALONG) for member in line[1:]]
    (
        self_queries, self_keys, self_values, self_powered, self_inverse, self_blend,
        self_attended, after_self, cross_queries,
    ) = self_forward(inputs[0], cross_row, *opened, self_output, cross_query)
    blocks = [member for pair in zip(line, line_beside) for member in pair]
    bits = 8
    while bits < devices:
        blocks = blocks + [permute(member, 0, bits) for member in blocks]
        bits *= 2
    if not shared:
        stacked = jnp.stack(blocks)
        order = jnp.arange(devices, dtype=jnp.int32) ^ lax.axis_index("mem")
        blocks = [jnp.take(stacked, order, axis=0).reshape(-1, width)]
        blocks = [blocks[0].reshape(devices, own_rows + 8, width)[at] for at in range(devices)]
    if shared:
        pool_memory, ids, *pool = memory_blocks(blocks, own_rows, encoder_row, cross_key, cross_value)
        keys, values, keys_t, values_t = (member[None] for member in pool)
    else:
        pool_memory = jnp.concatenate([member[:own_rows] for member in blocks], axis=0)
        pool_ids = jnp.concatenate([member[own_rows, :own_rows] for member in blocks], axis=0).astype(jnp.int32)
        pool_keys, pool_values, _, _ = memory_forward(pool_memory, encoder_row, cross_key, cross_value)
        passages = PASS_DEV * devices
        slot_rows, slot_visible = passage_slots(pool_ids, chosen, passages, pool_rows)
        keys = jnp.take(pool_keys, slot_rows, axis=0)
        values = jnp.take(pool_values, slot_rows, axis=0)
        keys_t, values_t = jnp.swapaxes(keys, 1, 2), jnp.swapaxes(values, 1, 2)
        ids = jnp.where(slot_visible, jnp.take(pool_ids, slot_rows), -1)
        ids = jnp.broadcast_to(ids[..., None], ids.shape + (SEQ,))
    cross_powered, cross_inverse, cross_blend, cross_attended = cross_forward(
        chosen, cross_queries, keys, values_t, ids
    )
    limits = jnp.minimum(target_lens[0], SEQ - task_ids[0] * (SEQ // 4))
    layer_out, grad_after_cross, grad_cross_attended, *turned = feed_both(
        limits, codes, after_self, cross_attended, cotangent[0], feed_row, cross_output, inner_weight, outer_weight
    )
    feed_sum = Sum(*turned)
    pieces = []
    for pair in range(PAIRS):
        piece = cross_backward(
            pair, grad_cross_attended, cross_queries, keys_t, values, cross_powered, cross_inverse, cross_blend
        )
        now = advance([feed_sum] if pair in (0, PAIRS - 1) else [], (grad_cross_attended, *piece))
        grad_cross_attended, pieces = now[0], pieces + [now[1:]]
    grad_keys, grad_values = [piece[1] for piece in pieces], [piece[2] for piece in pieces]
    if shared:
        pool_grads = [[member[0] for member in members] for members in (grad_keys, grad_values)]
    else:
        slot_index = jnp.where(slot_visible, slot_rows, pool_rows).reshape(-1)
        empty = jnp.zeros((pool_rows, PAIR), F32)
        pool_grads = [
            [empty.at[slot_index].add(member.reshape(-1, PAIR), mode="drop") for member in members]
            for members in (grad_keys, grad_values)
        ]
    made = memory_backward(own_rows, codes, pool_memory, encoder_row, cross_key, cross_value, *pool_grads)
    pulled = [piece[0] for piece in pieces]
    pulled[0], grad_pool_normed, pool_keep, pool_send = lax.optimization_barrier((pulled[0], *made))
    grad_own_normed = lax.psum_scatter(grad_pool_normed, "mem", scatter_dimension=0, tiled=True)
    made = cross_close(codes, pulled, after_self, grad_after_cross, cross_row, cross_query, self_attended)
    grad_after_self, query_keep, query_send, pool_keep, pool_send = advance([feed_sum], (*made, pool_keep, pool_send))
    cross_sum = Sum(
        jnp.concatenate([query_keep, pool_keep], axis=0), jnp.concatenate([query_send, pool_send], axis=0)
    )
    (half_pulled,) = self_backward(
        codes, None, grad_after_self, self_queries, self_keys, self_values, self_powered, self_inverse, self_blend,
        self_output, inputs[0], self_row,
    )
    grad_after_self, half_pulled = advance([feed_sum, cross_sum], (grad_after_self, half_pulled))
    made = self_backward(
        codes, half_pulled, grad_after_self, self_queries, self_keys, self_values, self_powered, self_inverse, self_blend,
        self_output, inputs[0], self_row,
    )
    grad_after_self, self_pulled, *turned = advance([feed_sum], (grad_after_self, *made))
    (feed_own,) = feed_sum.arrays
    gathered = lax.all_gather(feed_own, ("batch", "mem"), axis=0, tiled=False)
    if devices > 8:
        gathered = gathered.reshape((-1, devices) + feed_own.shape)[:, :8]
    gathered = gathered.reshape((-1, 8) + feed_own.shape)
    self_sum = Sum(*turned)
    (self_pulled,) = advance([self_sum], (self_pulled,))
    grad_inputs = self_close(self_pulled, grad_after_self, inputs[0], self_row, self_query, self_key, self_value)
    (grad_inputs,) = advance([cross_sum], (grad_inputs,))
    follow(cross_sum, self_sum)
    follow(self_sum, cross_sum)
    follow(cross_sum, self_sum)
    follow(self_sum, cross_sum)
    follow(cross_sum, self_sum)
    follow(self_sum, cross_sum)
    follow(cross_sum, self_sum)
    follow(self_sum, cross_sum)
    follow(self_sum, cross_sum)
    follow(cross_sum, self_sum)
    follow(cross_sum)
    (
        grad_cross_query, grad_self_output, grad_cross_key, grad_cross_value, grad_cross_gain, grad_encoder_gain,
    ) = restore_cross(
        codes, *cross_sum.arrays, cross_query, cross_key, cross_value, cross_row, encoder_row,
    )
    grad_cross_query, grad_own_normed, gathered = advance([self_sum], (grad_cross_query, grad_own_normed, gathered))
    steps = inner_weight.shape[1] // width
    grad_outer = restore_rows(gathered, 0, steps)
    grad_inner, grad_feed_gain = restore_columns(gathered, steps + 1, steps, inner_weight, feed_row)
    grad_cross_output = restore_rows(gathered, steps, 1)
    grad_self_query, grad_self_key, grad_self_value, grad_self_gain = restore_self(
        codes, *self_sum.arrays, self_query, self_key, self_value, self_row
    )
    memory_rows = memory[0].astype(F32)
    grad_memory = norm_pull(
        memory_rows, inverse_rms(memory_rows), encoder_row, grad_own_normed.astype(F32)
    )
    return (
        layer_out[None],
        grad_inputs[None],
        grad_memory[None],
        grad_encoder_gain[0],
        grad_self_gain[0],
        grad_cross_gain[0],
        grad_feed_gain[0],
        grad_self_query,
        grad_self_key,
        grad_self_value,
        grad_self_output,
        grad_cross_query,
        grad_cross_key,
        grad_cross_value,
        grad_cross_output,
        grad_inner,
        grad_outer,
    )


def solution(mesh):
    spread = (P("batch", "mem", None),) * 3
    in_specs = spread + (
        P("batch", "mem"), P("batch", "mem", None), P("batch", "mem"), P("batch", "mem"),
    ) + (P(),) * 14
    out_specs = spread + (P(),) * 14
    return jax.shard_map(local, mesh=mesh, in_specs=in_specs, out_specs=out_specs, check_vma=False)
```
